32 devices in a mesh: face: 2 (over x), tile: 16 (over z, y, core).
Axes of the slice: x: 2, y: 2, z: 4, core: 2. Of those that a mesh axis runs over, the one named last changes fastest.
Arguments:
- maps: bfloat16 [4, 4, 32, 2048], P(None, None, 'face', 'tile'), may hold values from -8 to 8
- params: float32 [4, 2], replicated, may hold values from 0 to 1
- labels: int32 [4], replicated, may hold values 0 or 1
- edge_flip: int32 [2, 16], replicated, may hold values from 0 to 1
- fine_weight: float32 [3, 4, 16], replicated, may hold values from -1.75 to 1.75
- coarse_weight: float32 [3, 16, 32], replicated, may hold values from -0.875 to 0.875
- feature_weight: float32 [32, 128], replicated, may hold values from -2 to 2
- param_weight: float32 [2, 128], replicated, may hold values from -4 to 4
- out_weight: float32 [128], replicated, may hold values from -1 to 1
Outputs:
- logits: float32 [4], replicated
- saliency: float32 [4, 4, 32, 2048], P(None, None, 'face', 'tile')
- grad_fine: float32 [3, 4, 16], replicated
- grad_coarse: float32 [3, 16, 32], replicated
The draws below stay inside these ranges and needn't reach their ends.
All inputs are finite; a program needn't handle non-finite values.
Results may differ from the reference program's by a relative error of at most 0.0003.
Values sent between devices are 32-bit elements; how exact they have to be, the bound alone decides.
A program may use at most 64 MiB of HBM per device.

```python
import jax
import jax.numpy as jnp
from jax import lax

BINS = 4
CH0 = 16
CH1 = 32
HIDDEN_UNITS = 128
NPAR = 2
ORDER = 3
MAPS = 4
R_DEV = 16
C_DEV = 128
ROWS = 32
COLS = 2048
FACES = 2
TILES = 16


def draw_maps(key, part):
    shape = (MAPS, BINS, ROWS, COLS)
    rows = (jnp.arange(ROWS, dtype=jnp.float32) + 0.5) / ROWS
    cols = (jnp.arange(COLS, dtype=jnp.float32) + 0.5) / COLS
    base = jnp.clip(jax.random.normal(key, shape, jnp.float32), -3.0, 3.0)
    profile = (0.6 + 1.4 * rows)[:, None] * (1.3 - 0.6 * cols)[None, :]
    values = base * profile
    return values.astype(jnp.bfloat16)


def touch_ends(entries, key, least, largest):
    shape = entries.shape
    index_at = [jax.random.randint(jax.random.fold_in(key, axis), (), 0, shape[axis]) for axis in range(len(shape))]
    entries = entries.at[tuple(index_at)].set(least)
    longest = shape.index(max(shape))
    index_at[longest] = (index_at[longest] + 1) % shape[longest]
    return entries.at[tuple(index_at)].set(largest)


def scatter_about(rng, dims, scale, limit, held_as=jnp.bfloat16):
    result = jax.random.normal(rng, dims, jnp.float32) * scale
    return jnp.minimum(jnp.maximum(result, -limit), limit).astype(held_as)


def setup_inputs(seed: int = 0) -> dict:
    key_list = jax.random.split(jax.random.key(seed), 10)
    maps = draw_maps(jax.random.fold_in(key_list[9], 71), 0)
    params = jnp.clip(jax.random.uniform(key_list[1], (MAPS, NPAR), jnp.float32, 0.0, 1.0), 0.0, 1.0)
    labels = touch_ends((jax.random.randint(key_list[2], (MAPS,), 0, 2) < 1).astype(jnp.int32), jax.random.fold_in(key_list[2], 1), 0, 1)
    edge_flip = touch_ends(jax.random.randint(key_list[3], (FACES, TILES), 0, 2), jax.random.fold_in(key_list[3], 1), 0, 1).astype(jnp.int32)
    fine_weight = scatter_about(key_list[4], (ORDER, BINS, CH0), (ORDER * BINS) ** -0.5, 1.75, jnp.float32)
    coarse_weight = scatter_about(key_list[5], (ORDER, CH0, CH1), (ORDER * CH0) ** -0.5, 0.875, jnp.float32)
    feature_weight = scatter_about(key_list[6], (CH1, HIDDEN_UNITS), (CH1 // 4) ** -0.5, 2.0, jnp.float32)
    param_weight = scatter_about(key_list[7], (NPAR, HIDDEN_UNITS), NPAR ** -0.5, 4.0, jnp.float32)
    out_weight = scatter_about(key_list[8], (HIDDEN_UNITS,), (HIDDEN_UNITS // 4) ** -0.5, 1.0, jnp.float32)
    return {"maps": maps, "params": params, "labels": labels, "edge_flip": edge_flip, "fine_weight": fine_weight, "coarse_weight": coarse_weight, "feature_weight": feature_weight, "param_weight": param_weight, "out_weight": out_weight}


exact = lax.Precision.HIGHEST


def lap(field, edge_flip, block_rows, block_cols):
    nrows = field.shape[-2]
    ncols = field.shape[-1]
    turned = field.reshape(field.shape[:-1] + (ncols // block_cols, block_cols))[..., ::-1].reshape(field.shape)
    rows = jnp.arange(nrows)
    cols = jnp.arange(ncols)
    block = rows // block_rows
    colblock = cols // block_cols
    faces = edge_flip.shape[0]
    top_flags = edge_flip[block][:, colblock] == 1
    bottom_flags = edge_flip[(block + 1) % faces][:, colblock] == 1
    top_mask = (rows % block_rows == 0)[:, None] & top_flags
    bottom_mask = (rows % block_rows == block_rows - 1)[:, None] & bottom_flags
    upper = jnp.where(top_mask, jnp.roll(turned, 1, -2), jnp.roll(field, 1, -2))
    lower = jnp.where(bottom_mask, jnp.roll(turned, -1, -2), jnp.roll(field, -1, -2))
    return -0.25 * (upper + lower + jnp.roll(field, 1, -1) + jnp.roll(field, -1, -1))


def cheb_terms(field, edge_flip, block_rows, block_cols):
    first = lap(field, edge_flip, block_rows, block_cols)
    second = 2.0 * lap(first, edge_flip, block_rows, block_cols) - field
    return jnp.stack([field, first, second])


def cheb_adjoint(parts, edge_flip, block_rows, block_cols):
    inner = lap(parts[2], edge_flip, block_rows, block_cols)
    outer = lap(parts[1] + 2.0 * inner, edge_flip, block_rows, block_cols)
    return parts[0] - parts[2] + outer


def reference(maps, params, labels, edge_flip, fine_weight, coarse_weight, feature_weight, param_weight, out_weight):
    pooled_count = (ROWS // 2) * (COLS // 2)

    def forward_map(single):
        x0 = single.astype(jnp.float32)
        terms0 = cheb_terms(x0, edge_flip, R_DEV, C_DEV)
        pre0 = jnp.einsum("kio,kirc->orc", fine_weight, terms0, precision=exact)
        act0 = jax.nn.softplus(pre0)
        x1 = act0.reshape(CH0, ROWS // 2, 2, COLS // 2, 2).mean(axis=(2, 4))
        terms1 = cheb_terms(x1, edge_flip, R_DEV // 2, C_DEV // 2)
        pre1 = jnp.einsum("kio,kirc->orc", coarse_weight, terms1, precision=exact)
        return terms0, pre0, terms1, pre1

    def feature_map(single):
        pre1 = forward_map(single)[3]
        return jax.nn.softplus(pre1).sum(axis=(1, 2))

    features = lax.map(feature_map, maps) / pooled_count
    hidden = jnp.tanh(jnp.dot(features, feature_weight, precision=exact) + jnp.dot(params, param_weight, precision=exact))
    logits = jnp.dot(hidden, out_weight, precision=exact)
    dlogit = jax.nn.sigmoid(logits) - labels.astype(jnp.float32)
    dhidden = dlogit[:, None] * out_weight[None, :] * (1.0 - hidden * hidden)
    dfeatures = jnp.dot(dhidden, feature_weight.T, precision=exact)

    def backward_map(pair):
        single, dfeat = pair
        terms0, pre0, terms1, pre1 = forward_map(single)
        dpre1 = (dfeat / pooled_count)[:, None, None] * jax.nn.sigmoid(pre1)
        grad_c = jnp.einsum("kirc,orc->kio", terms1, dpre1, precision=exact)
        parts1 = jnp.einsum("kio,orc->kirc", coarse_weight, dpre1, precision=exact)
        dx1 = cheb_adjoint(parts1, edge_flip, R_DEV // 2, C_DEV // 2)
        spread = jnp.broadcast_to(dx1[:, :, None, :, None], (CH0, ROWS // 2, 2, COLS // 2, 2)).reshape(pre0.shape)
        dpre0 = 0.25 * spread * jax.nn.sigmoid(pre0)
        grad_f = jnp.einsum("kirc,orc->kio", terms0, dpre0, precision=exact)
        parts0 = jnp.einsum("kio,orc->kirc", fine_weight, dpre0, precision=exact)
        dx0 = cheb_adjoint(parts0, edge_flip, R_DEV, C_DEV)
        return dx0 * (ROWS * COLS), grad_f, grad_c

    saliency, grad_f, grad_c = lax.map(backward_map, (maps, dfeatures))
    return logits, saliency, grad_f.sum(axis=0), grad_c.sum(axis=0)
```

```python
import functools

import jax
import jax.numpy as jnp
from jax import lax
from jax.experimental import pallas as pl
from jax.experimental.pallas import tpu as pltpu
from jax.sharding import PartitionSpec as P

f32 = jnp.float32
exact = lax.Precision.HIGHEST
MESH = pl.DeviceIdType.MESH
LANES = 128
HALF = 64
UP, DOWN, LEFT, RIGHT, UL, UR, DL, DR = range(8)


def mm(a, b, ca=1, cb=0, precision=exact):
    return lax.dot_general(
        a, b, (((ca,), (cb,)), ((), ())), precision=precision, preferred_element_type=f32
    )


def iota(shape, dim):
    return lax.broadcasted_iota(jnp.int32, shape, dim)


def onehot(cond):
    return jnp.where(cond, 1.0, 0.0).astype(f32)


def swap(x):
    return pltpu.roll(x, HALF, axis=x.ndim - 1)


def pick(flag, yes, no):
    return flag * yes + (1.0 - flag) * no


def from_left(x, edge):
    axis = x.ndim - 2
    return jnp.where(iota(x.shape, axis) == 0, edge, pltpu.roll(x, 1, axis=axis))


def from_right(x, edge):
    axis = x.ndim - 2
    n = x.shape[axis]
    return jnp.where(iota(x.shape, axis) == n - 1, edge, pltpu.roll(x, n - 1, axis=axis))


def beside(x, left, right, fine):
    if not fine:
        return from_left(x, left) + from_right(x, right)
    s = swap(x)
    even = iota(x.shape, x.ndim - 1) < HALF
    return s + jnp.where(even, from_left(s, swap(left)), from_right(s, swap(right)))


def lap(x, up, down, left, right, fine):
    above = jnp.concatenate([up[None], x[:-1]], axis=0)
    below = jnp.concatenate([x[1:], down[None]], axis=0)
    return -0.25 * (above + below + beside(x, left, right, fine))


class Exchange:
    def __init__(self, field, bufs, send_sem, recv_sem, place, fine):
        self.field, self.place, self.fine = field, place, fine
        self.row_recv, self.col_send, self.col_recv, self.end_send, self.end_recv = bufs
        self.send_sem, self.recv_sem = send_sem, recv_sem

    def start(self):
        field, (face, tile, faces, tiles) = self.field, self.place
        nrows, ncols, _ = field.shape
        up, down = lax.rem(face + faces - 1, faces), lax.rem(face + 1, faces)
        left, right = lax.rem(tile + tiles - 1, tiles), lax.rem(tile + 1, tiles)
        copies = [None] * 8

        def send(way, src, dst, target):
            copies[way] = pltpu.make_async_remote_copy(
                src_ref=src,
                dst_ref=dst,
                send_sem=self.send_sem.at[way],
                recv_sem=self.recv_sem.at[way],
                device_id=target,
                device_id_type=MESH,
            )
            copies[way].start()

        send(UP, field.at[pl.ds(0, 2)], self.row_recv.at[1], (up, tile))
        send(DOWN, field.at[pl.ds(nrows - 2, 2)], self.row_recv.at[0], (down, tile))
        width = self.col_send.shape[1]
        for w in range(width):
            self.col_send[0, w] = field[:, w : w + 1, :]
            self.col_send[1, w] = field[:, ncols - 1 - w : ncols - w, :]
        for side, row in ((0, 0), (1, nrows - 1)):
            self.end_send[side, 0] = field[row, 0:1, :]
            self.end_send[side, 1] = field[row, ncols - 1 : ncols, :]
        send(LEFT, self.col_send.at[0], self.col_recv.at[1], (face, left))
        send(RIGHT, self.col_send.at[1], self.col_recv.at[0], (face, right))
        send(UL, self.end_send.at[0], self.end_recv.at[3], (up, left))
        send(UR, self.end_send.at[0], self.end_recv.at[2], (up, right))
        send(DL, self.end_send.at[1], self.end_recv.at[1], (down, left))
        send(DR, self.end_send.at[1], self.end_recv.at[0], (down, right))
        self.copies = copies

    def turn(self, x):
        return swap(x) if self.fine else x

    def outer(self, flags, rows, end_left, end_right):
        flag_left, flag, flag_right = flags
        ncols = rows.shape[1]
        mirror = onehot(iota((ncols, ncols), 0) + iota((ncols, ncols), 1) == ncols - 1)
        pair = jnp.concatenate([rows[0], rows[1]], axis=1)
        turned = mm(mirror, pair)
        rows = [
            pick(flag, self.turn(turned[:, LANES * i : LANES * (i + 1)]), rows[i]) for i in range(2)
        ]
        row_left = pick(flag, self.turn(end_right[0]), end_left[1])
        row_right = pick(flag, self.turn(end_left[1]), end_right[0])
        col_left = pick(flag_left, self.turn(end_left[0]), end_left[1])
        col_right = pick(flag_right, self.turn(end_right[1]), end_right[0])
        return rows, row_left, row_right, col_left, col_right

    def finish(self, flags_up, flags_down):
        for copy in self.copies:
            copy.wait()
        fine = self.fine
        x = self.field[...]
        nrows, ncols, _ = x.shape
        ends = self.end_recv[...]
        (u2, u1), ul, ur, lu, ru = self.outer(flags_up, self.row_recv[0], ends[0], ends[1])
        (d1, d2), dl, dr, ld, rd = self.outer(flags_down, self.row_recv[1], ends[2], ends[3])
        lefts, rights = self.col_recv[0], self.col_recv[1]
        first = lap(x, u1, d1, lefts[0], rights[0], fine)
        first_u = -0.25 * (u2 + x[0] + beside(u1, ul, ur, fine))
        first_d = -0.25 * (d2 + x[nrows - 1] + beside(d1, dl, dr, fine))
        if fine:
            along_l = swap(lefts[0]) + swap(self.field[:, 0:1, :])
            along_r = swap(rights[0]) + swap(self.field[:, ncols - 1 : ncols, :])
        else:
            along_l = lefts[1] + self.field[:, 0:1, :]
            along_r = rights[1] + self.field[:, ncols - 1 : ncols, :]

        def edge(col, over, under, along):
            above = jnp.concatenate([over[None], col[:-1]], axis=0)
            below = jnp.concatenate([col[1:], under[None]], axis=0)
            return -0.25 * (above + below + along)

        first_l = edge(lefts[0], lu, ld, along_l)
        first_r = edge(rights[0], ru, rd, along_r)
        second = 2.0 * lap(first, first_u, first_d, first_l, first_r, fine) - x
        return first, second


class GroupSum:
    def __init__(self, slots, sems, me, device_of):
        self.slots, self.sems, self.me, self.device_of = slots, sems, me, device_of
        self.count = slots.shape[0]

    def start(self, value):
        me, count = self.me, self.count
        self.slots[me] = value

        def step(k, _):
            pltpu.make_async_remote_copy(
                src_ref=self.slots.at[me],
                dst_ref=self.slots.at[me],
                send_sem=self.sems.at[0],
                recv_sem=self.sems.at[1],
                device_id=self.device_of(lax.rem(me + k, count)),
                device_id_type=MESH,
            ).start()
            return 0

        lax.fori_loop(1, count, step, 0)

    def finish(self):
        others = self.slots.at[pl.ds(0, self.count - 1)]
        pltpu.make_async_copy(others, others, self.sems.at[1]).wait()
        pltpu.make_async_copy(others, others, self.sems.at[0]).wait()
        total = self.slots[0]
        if self.count <= 8:
            for i in range(1, self.count):
                total = total + self.slots[i]
            return total
        return jnp.sum(self.slots[...], axis=0)


def kernel(
    faces,
    tiles,
    maps_ref,
    params_ref,
    labels_ref,
    flip_ref,
    fine_ref,
    coarse_ref,
    feature_ref,
    param_w_ref,
    out_w_ref,
    logits_ref,
    sal_ref,
    grad_f_ref,
    grad_c_ref,
    x0_ref,
    t0_ref,
    sig0_ref,
    x1_ref,
    t1_ref,
    d1_ref,
    d0_ref,
    sal_t_ref,
    fine_rows,
    fine_col_send,
    fine_col_recv,
    coarse_rows,
    coarse_col_send,
    coarse_col_recv,
    end_send,
    end_recv,
    halo_send,
    halo_recv,
    feature_slots,
    face_slots,
    low_slots,
    high_slots,
    sum_sems,
):
    face, tile = lax.axis_index("face"), lax.axis_index("tile")
    place = (face, tile, faces, tiles)
    devices = faces * tiles
    linear = face * tiles + tile
    nbins, nch0 = fine_ref.shape[1:]
    nch1 = coarse_ref.shape[2]
    nmaps = params_ref.shape[0]
    order = fine_ref.shape[0]
    nrows = maps_ref.shape[0]
    ncols = maps_ref.shape[2] // 2
    fields = nmaps * nbins
    pooled = float(nrows // 2 * ncols * devices)

    def device_of(i):
        return (lax.div(i, tiles), lax.rem(i, tiles))

    barrier = pltpu.get_barrier_semaphore()

    def greet(k, _):
        pl.semaphore_signal(
            barrier,
            inc=1,
            device_id=device_of(lax.rem(linear + k, devices)),
            device_id_type=MESH,
        )
        return 0

    lax.fori_loop(1, devices, greet, 0)

    col = iota((ncols, 2 * ncols), 1)
    pairs = [
        onehot(col == 2 * iota((ncols, 2 * ncols), 0) + p).astype(jnp.bfloat16) for p in range(2)
    ]

    zero = jnp.zeros((HALF - fields, 2 * ncols), jnp.bfloat16)

    def load_row(r, _):
        row = jnp.concatenate([maps_ref[r], zero], axis=0)
        halves = [mm(pairs[p], row, 1, 1, None) for p in range(2)]
        x0_ref[r] = jnp.concatenate(halves, axis=1)
        return 0

    lax.fori_loop(0, nrows, load_row, 0)
    pl.semaphore_wait(barrier, devices - 1)

    def exchange(i, field, fine):
        rows, sends, recvs = (
            (fine_rows, fine_col_send, fine_col_recv)
            if fine
            else (coarse_rows, coarse_col_send, coarse_col_recv)
        )
        slot = i // 2
        bufs = (rows.at[slot], sends.at[slot], recvs.at[slot], end_send.at[i], end_recv.at[i])
        return Exchange(field, bufs, halo_send.at[i], halo_recv.at[i], place, fine)

    ex0 = exchange(0, x0_ref, True)
    ex0.start()

    below = lax.rem(face + 1, faces)
    spots = (lax.rem(tile + tiles - 1, tiles), tile, lax.rem(tile + 1, tiles))
    flags_up = [jnp.where(flip_ref[face, s] == 1, 1.0, 0.0).astype(f32) for s in spots]
    flags_down = [jnp.where(flip_ref[below, s] == 1, 1.0, 0.0).astype(f32) for s in spots]

    square = (LANES, LANES)
    ri, ci = iota(square, 0), iota(square, 1)
    mask0 = onehot(
        (ri // HALF == ci // HALF)
        & (ri % HALF < fields)
        & ((ri % HALF) // nbins == (ci % HALF) // nch0)
    )
    mask1 = onehot((ri % HALF) // nch0 == ci // nch1)
    at_bin = onehot(iota((LANES, nbins), 0) % nbins == iota((LANES, nbins), 1))
    at_ch0 = onehot(iota((nch0, LANES), 1) % nch0 == iota((nch0, LANES), 0))
    at_ch1 = onehot(iota((nch1, LANES), 1) % nch1 == iota((nch1, LANES), 0))
    w0 = [mask0 * mm(mm(at_bin, fine_ref[k]), at_ch0) for k in range(order)]
    w1 = [mask1 * mm(mm(at_ch0, coarse_ref[k], 0, 0), at_ch1) for k in range(order)]
    wf = mm(at_ch1, feature_ref[...], 0, 0)
    head_mask = onehot(iota((nmaps, LANES), 0) == iota((nmaps, LANES), 1) // nch1)

    first, second = ex0.finish(flags_up, flags_down)
    t0_ref[0] = first
    t0_ref[1] = second

    def flat(x):
        return x.reshape(-1, LANES)

    def conv(terms, weights, cb):
        total = mm(flat(terms[0]), weights[0], 1, cb)
        for k in range(1, order):
            total = total + mm(flat(terms[k]), weights[k], 1, cb)
        return total

    pre0 = conv((x0_ref[...], first, second), w0, 0)
    small = jnp.exp(-jnp.abs(pre0))
    act0 = jnp.maximum(pre0, 0.0) + jnp.log1p(small)
    sig0_ref[...] = (0.25 * jnp.where(pre0 >= 0, 1.0, small) / (1.0 + small)).reshape(
        nrows, ncols, LANES
    )
    act0 = act0.reshape(nrows // 2, 2, ncols, LANES)
    x1_ref[...] = 0.25 * (act0[:, 0] + act0[:, 1])

    ex1 = exchange(1, x1_ref, False)
    ex1.start()
    first, second = ex1.finish(flags_up, flags_down)
    t1_ref[0] = first
    t1_ref[1] = second
    pre1 = conv((x1_ref[...], first, second), w1, 0)
    small = jnp.exp(-jnp.abs(pre1))
    act1 = jnp.maximum(pre1, 0.0) + jnp.log1p(small)
    feature_sum = GroupSum(feature_slots, sum_sems.at[0], linear, device_of)
    feature_sum.start(jnp.sum(act1, axis=0, keepdims=True))
    sig1 = jnp.where(pre1 >= 0, 1.0, small) / (1.0 + small)
    from_params = params_ref[:, 0:1] * param_w_ref[0:1, :]
    for i in range(1, params_ref.shape[1]):
        from_params = from_params + params_ref[:, i : i + 1] * param_w_ref[i : i + 1, :]
    features = feature_sum.finish() / pooled
    hidden = jnp.tanh(mm(head_mask * features, wf) + from_params)
    logits = jnp.sum(hidden * out_w_ref[...], axis=1, keepdims=True)
    logits_ref[...] = logits
    dlogit = 1.0 / (1.0 + jnp.exp(-logits)) - labels_ref[...].astype(f32)
    dhidden = dlogit * out_w_ref[...] * (1.0 - hidden * hidden)
    dfeatures = jnp.sum(head_mask * mm(dhidden, wf, 1, 1), axis=0, keepdims=True)
    dpre1 = (dfeatures / pooled) * sig1
    d1_ref[...] = dpre1.reshape(nrows // 2, ncols, LANES)

    ex2 = exchange(2, d1_ref, False)
    ex2.start()

    grads = jnp.zeros((nch0, LANES), f32)
    for k in range(order):
        term = x1_ref[...] if k == 0 else t1_ref[k - 1]
        full = mask1 * mm(flat(term), dpre1, 0, 0)
        to_lane = onehot(ri % nch1 + k * nch1 == ci)
        grads = grads + mm(mm(at_ch0, full), to_lane)

    first, second = ex2.finish(flags_up, flags_down)
    dx1 = conv((d1_ref[...], first, second), w1, 1).reshape(nrows // 2, 1, ncols, LANES)
    sig0 = sig0_ref[...].reshape(nrows // 2, 2, ncols, LANES)
    d0_ref[...] = (dx1 * sig0).reshape(nrows, ncols, LANES)

    ex3 = exchange(3, d0_ref, True)
    ex3.start()
    dpre0 = flat(d0_ref[...])
    to_lane = onehot(ri % nch0 + order * nch1 == ci)
    for k in range(order):
        term = x0_ref[...] if k == 0 else t0_ref[k - 1]
        full = mask0 * mm(flat(term), dpre0, 0, 0)
        row, lane = iota((nch0, LANES), 0), iota((nch0, LANES), 1)
        to_row = onehot(lane % nbins + k * nbins == row)
        grads = grads + mm(mm(to_row, full), to_lane)

    low = low_slots.shape[0]
    tile_high, tile_low = lax.div(tile, low), lax.rem(tile, low)
    sums = [
        GroupSum(low_slots, sum_sems.at[1], tile_low, lambda j: (face, tile_high * low + j)),
        GroupSum(face_slots, sum_sems.at[2], face, lambda j: (j, tile)),
        GroupSum(high_slots, sum_sems.at[3], tile_high, lambda j: (face, j * low + tile_low)),
    ]
    sums[0].start(grads)
    first, second = ex3.finish(flags_up, flags_down)
    sums[1].start(sums[0].finish())
    pixels = float(nrows * faces * 2 * ncols * tiles)
    saliency = pixels * conv((d0_ref[...], first, second), w0, 1)
    sal_t_ref[...] = saliency.reshape(nrows, ncols, LANES)
    sums[2].start(sums[1].finish())
    wide = [p.astype(f32) for p in pairs]

    def store_row(r, _):
        row = sal_t_ref[r]
        total = mm(row, wide[0], 0, 0)[0:fields] + mm(row, wide[1], 0, 0)[HALF : HALF + fields]
        sal_ref[r] = total
        return 0

    lax.fori_loop(0, nrows, store_row, 0)
    grads = sums[2].finish()
    for k in range(order):
        grad_c_ref[k] = grads[:, k * nch1 : (k + 1) * nch1]
        start = order * nch1
        grad_f_ref[k] = grads[k * nbins : (k + 1) * nbins, start : start + nch0]


def on_device(faces, tiles, maps, params, labels, flip, fine_w, coarse_w, feature_w, param_w, out_w):
    nmaps, nbins, nrows, width = maps.shape
    ncols = width // 2
    low = 1
    while low * low < tiles:
        low *= 2
    vmem = pl.BlockSpec(memory_space=pltpu.VMEM)
    smem = pl.BlockSpec(memory_space=pltpu.SMEM)
    fine = (nrows, ncols, LANES)
    coarse = (nrows // 2, ncols, LANES)

    def buf(*shape):
        return pltpu.VMEM(shape, f32)

    logits, saliency, grad_f, grad_c = pl.pallas_call(
        functools.partial(kernel, faces, tiles),
        out_shape=(
            jax.ShapeDtypeStruct((nmaps, 1), f32),
            jax.ShapeDtypeStruct((nrows, nmaps * nbins, width), f32),
            jax.ShapeDtypeStruct(fine_w.shape, f32),
            jax.ShapeDtypeStruct(coarse_w.shape, f32),
        ),
        in_specs=[vmem, vmem, vmem, smem, vmem, vmem, vmem, vmem, vmem],
        out_specs=(vmem,) * 4,
        scratch_shapes=[
            buf(*fine),
            buf(2, *fine),
            buf(*fine),
            buf(*coarse),
            buf(2, *coarse),
            buf(*coarse),
            buf(*fine),
            buf(*fine),
            buf(2, 2, 2, ncols, LANES),
            buf(2, 2, 1, nrows, 1, LANES),
            buf(2, 2, 1, nrows, 1, LANES),
            buf(2, 2, 2, ncols, LANES),
            buf(2, 2, 2, nrows // 2, 1, LANES),
            buf(2, 2, 2, nrows // 2, 1, LANES),
            buf(4, 2, 2, 1, LANES),
            buf(4, 4, 2, 1, LANES),
            pltpu.SemaphoreType.DMA((4, 8)),
            pltpu.SemaphoreType.DMA((4, 8)),
            buf(faces * tiles, 1, LANES),
            buf(faces, fine_w.shape[2], LANES),
            buf(low, fine_w.shape[2], LANES),
            buf(tiles // low, fine_w.shape[2], LANES),
            pltpu.SemaphoreType.DMA((4, 2)),
        ],
        compiler_params=pltpu.CompilerParams(
            collective_id=0, has_side_effects=True, vmem_limit_bytes=48 * 1024 * 1024
        ),
    )(
        maps.reshape(nmaps * nbins, nrows, width).transpose(1, 0, 2),
        params,
        labels.reshape(nmaps, 1),
        flip,
        fine_w,
        coarse_w,
        feature_w,
        param_w,
        out_w.reshape(1, -1),
    )
    saliency = saliency.transpose(1, 0, 2).reshape(maps.shape)
    return logits.reshape(nmaps), saliency, grad_f, grad_c


def solution(mesh):
    in_specs = (P(None, None, "face", "tile"), P(), P(), P(), P(), P(), P(), P(), P())
    out_specs = (P(), P(None, None, "face", "tile"), P(), P())
    body = functools.partial(on_device, mesh.shape["face"], mesh.shape["tile"])
    return jax.shard_map(body, mesh=mesh, in_specs=in_specs, out_specs=out_specs, check_vma=False)
```

```python
import functools

import jax
import jax.numpy as jnp
from jax import lax
from jax.experimental import pallas as pl
from jax.experimental.pallas import tpu as pltpu
from jax.sharding import PartitionSpec as P

f32 = jnp.float32
bf16 = jnp.bfloat16
exact = lax.Precision.HIGHEST
MESH = pl.DeviceIdType.MESH
LANES = 128
HALF = 64
UP, DOWN, LEFT, RIGHT, UL, UR, DL, DR = range(8)


def mm(a, b, ca=1, cb=0, precision=exact):
    return lax.dot_general(
        a, b, (((ca,), (cb,)), ((), ())), precision=precision, preferred_element_type=f32
    )


def split(x):
    high = x.astype(bf16)
    return high, (x - high.astype(f32)).astype(bf16)


def mm3(a, b, ca=1, cb=0):
    (ah, al), (bh, bl) = a, b
    left = jnp.concatenate([ah, al, ah], axis=ca)
    right = jnp.concatenate([bh, bh, bl], axis=cb)
    return mm(left, right, ca, cb, None)


def iota(shape, dim):
    return lax.broadcasted_iota(jnp.int32, shape, dim)


def onehot(cond):
    return jnp.where(cond, 1.0, 0.0).astype(f32)


def swap(x):
    return pltpu.roll(x, HALF, axis=x.ndim - 1)


def pick(flag, yes, no):
    return flag * yes + (1.0 - flag) * no


def from_left(x, edge):
    axis = x.ndim - 2
    return jnp.where(iota(x.shape, axis) == 0, edge, pltpu.roll(x, 1, axis=axis))


def from_right(x, edge):
    axis = x.ndim - 2
    n = x.shape[axis]
    return jnp.where(iota(x.shape, axis) == n - 1, edge, pltpu.roll(x, n - 1, axis=axis))


def beside(x, left, right, fine):
    if not fine:
        return from_left(x, left) + from_right(x, right)
    s = swap(x)
    even = iota(x.shape, x.ndim - 1) < HALF
    return s + jnp.where(even, from_left(s, swap(left)), from_right(s, swap(right)))


def lap(x, up, down, left, right, fine):
    above = jnp.concatenate([up[None], x[:-1]], axis=0)
    below = jnp.concatenate([x[1:], down[None]], axis=0)
    return -0.25 * (above + below + beside(x, left, right, fine))


def lane_block(shape, size):
    return (iota(shape, len(shape) - 1) % HALF) // size


def pack_input(size, near, far):
    pair = near + pltpu.roll(far, size, axis=1)
    n = pair.shape[0] // 2
    return pair[:n] + pltpu.roll(pair[n:], 2 * size, axis=1)


def unpack_input(size, packed):
    def block(i):
        here = packed if i == 0 else pltpu.roll(packed, LANES - i * size, axis=1)
        return jnp.where(lane_block(here.shape, size) == 0, here, 0.0)

    near = jnp.concatenate([block(0), block(2)], axis=0)
    far = jnp.concatenate([block(1), block(3)], axis=0)
    return near, far


def pack_pooled(near, far):
    low = iota(near.shape, 1) < HALF
    return jnp.where(low, near + swap(near), far + swap(far))


def unpack_pooled(packed):
    low = iota(packed.shape, 1) < HALF
    return jnp.where(low, packed, 0.0), jnp.where(low, 0.0, packed)


def pack_mixed(size, near, far):
    return jnp.where(
        lane_block(near.shape, size) == 3, pltpu.roll(far, size, axis=1), near
    )


def unpack_mixed(size, packed):
    return packed, pltpu.roll(packed, LANES - size, axis=1)


class Exchange:
    def __init__(self, field, bufs, send_sem, recv_sem, place, fine, pack, unpack):
        self.field, self.place, self.fine = field, place, fine
        self.pack, self.unpack = pack, unpack
        self.row_send, self.row_recv = bufs[:2]
        self.col_send, self.col_recv, self.end_send, self.end_recv = bufs[2:]
        self.send_sem, self.recv_sem = send_sem, recv_sem

    def start(self):
        field, (face, tile, faces, tiles) = self.field, self.place
        nrows, ncols, _ = field.shape
        up, down = lax.rem(face + faces - 1, faces), lax.rem(face + 1, faces)
        left, right = lax.rem(tile + tiles - 1, tiles), lax.rem(tile + 1, tiles)
        copies = [None] * 8

        def send(way, src, dst, target):
            copies[way] = pltpu.make_async_remote_copy(
                src_ref=src,
                dst_ref=dst,
                send_sem=self.send_sem.at[way],
                recv_sem=self.recv_sem.at[way],
                device_id=target,
                device_id_type=MESH,
            )
            copies[way].start()

        if self.pack is None:
            send(UP, field.at[pl.ds(0, 2)], self.row_recv.at[1], (up, tile))
            send(DOWN, field.at[pl.ds(nrows - 2, 2)], self.row_recv.at[0], (down, tile))
        else:
            self.row_send[0] = self.pack(field[0], field[1])
            send(UP, self.row_send.at[0], self.row_recv.at[1], (up, tile))
            self.row_send[1] = self.pack(field[nrows - 1], field[nrows - 2])
            send(DOWN, self.row_send.at[1], self.row_recv.at[0], (down, tile))
        for side, row in ((0, 0), (1, nrows - 1)):
            self.end_send[side, 0] = field[row, 0:1, :]
            self.end_send[side, 1] = field[row, ncols - 1 : ncols, :]
        send(UL, self.end_send.at[0], self.end_recv.at[3], (up, left))
        send(UR, self.end_send.at[0], self.end_recv.at[2], (up, right))
        send(DL, self.end_send.at[1], self.end_recv.at[1], (down, left))
        send(DR, self.end_send.at[1], self.end_recv.at[0], (down, right))
        width = self.col_send.shape[1]
        for w in range(width):
            self.col_send[0, w] = field[:, w : w + 1, :]
            self.col_send[1, w] = field[:, ncols - 1 - w : ncols - w, :]
        send(LEFT, self.col_send.at[0], self.col_recv.at[1], (face, left))
        send(RIGHT, self.col_send.at[1], self.col_recv.at[0], (face, right))
        self.copies = copies

    def rows(self, side):
        got = self.row_recv[side]
        if self.pack is None:
            return (got[1], got[0]) if side == 0 else (got[0], got[1])
        return self.unpack(got)

    def turn(self, x):
        return swap(x) if self.fine else x

    def outer(self, flags, rows, end_left, end_right):
        flag_left, flag, flag_right = flags
        ncols = rows[0].shape[0]
        at = (ncols, 2 * ncols)
        mirror = onehot(iota(at, 0) + iota(at, 1) % ncols == ncols - 1).astype(bf16)
        pair = jnp.concatenate(split(jnp.concatenate(rows, axis=1)), axis=0)
        turned = mm(mirror, pair, 1, 0, None)
        rows = [
            pick(flag, self.turn(turned[:, LANES * i : LANES * (i + 1)]), rows[i]) for i in range(2)
        ]
        row_left = pick(flag, self.turn(end_right[0]), end_left[1])
        row_right = pick(flag, self.turn(end_left[1]), end_right[0])
        col_left = pick(flag_left, self.turn(end_left[0]), end_left[1])
        col_right = pick(flag_right, self.turn(end_right[1]), end_right[0])
        return rows, row_left, row_right, col_left, col_right

    def finish(self, flags_up, flags_down, mix=None):
        for copy in self.copies:
            copy.wait()
        fine = self.fine
        x = self.field[...]
        nrows, ncols, _ = x.shape
        ends = self.end_recv[...]
        (u1, u2), ul, ur, lu, ru = self.outer(flags_up, self.rows(0), ends[0], ends[1])
        (d1, d2), dl, dr, ld, rd = self.outer(flags_down, self.rows(1), ends[2], ends[3])
        lefts, rights = self.col_recv[0], self.col_recv[1]
        first = lap(x, u1, d1, lefts[0], rights[0], fine)
        first_u = -0.25 * (u2 + x[0] + beside(u1, ul, ur, fine))
        first_d = -0.25 * (d2 + x[nrows - 1] + beside(d1, dl, dr, fine))
        if fine:
            along_l = swap(lefts[0]) + swap(self.field[:, 0:1, :])
            along_r = swap(rights[0]) + swap(self.field[:, ncols - 1 : ncols, :])
        else:
            along_l = lefts[1] + self.field[:, 0:1, :]
            along_r = rights[1] + self.field[:, ncols - 1 : ncols, :]

        def edge(col, over, under, along):
            above = jnp.concatenate([over[None], col[:-1]], axis=0)
            below = jnp.concatenate([col[1:], under[None]], axis=0)
            return -0.25 * (above + below + along)

        first_l = edge(lefts[0], lu, ld, along_l)
        first_r = edge(rights[0], ru, rd, along_r)
        if mix is None:
            return first, 2.0 * lap(first, first_u, first_d, first_l, first_r, fine) - x
        return first, lap(
            mix(x, first),
            mix(u1, first_u),
            mix(d1, first_d),
            mix(lefts[0], first_l),
            mix(rights[0], first_r),
            fine,
        )


class GroupSum:
    def __init__(self, slots, sems, me, device_of):
        self.slots, self.sems, self.me, self.device_of = slots, sems, me, device_of
        self.count = slots.shape[0]

    def start(self, value):
        me, count = self.me, self.count
        self.slots[me] = value

        def step(k, _):
            pltpu.make_async_remote_copy(
                src_ref=self.slots.at[me],
                dst_ref=self.slots.at[me],
                send_sem=self.sems.at[0],
                recv_sem=self.sems.at[1],
                device_id=self.device_of(lax.rem(me + k, count)),
                device_id_type=MESH,
            ).start()
            return 0

        lax.fori_loop(1, count, step, 0)

    def finish(self):
        others = self.slots.at[pl.ds(0, self.count - 1)]
        pltpu.make_async_copy(others, others, self.sems.at[1]).wait()
        pltpu.make_async_copy(others, others, self.sems.at[0]).wait()
        total = self.slots[0]
        if self.count <= 8:
            for i in range(1, self.count):
                total = total + self.slots[i]
            return total
        return jnp.sum(self.slots[...], axis=0)


def kernel(
    faces,
    tiles,
    maps_ref,
    params_ref,
    labels_ref,
    flip_ref,
    fine_ref,
    coarse_ref,
    feature_ref,
    param_w_ref,
    out_w_ref,
    logits_ref,
    sal_ref,
    grad_f_ref,
    grad_c_ref,
    x0_ref,
    t0_ref,
    sig0_ref,
    x1_ref,
    t1_ref,
    d1_ref,
    d0_ref,
    flat_ref,
    input_rows_send,
    input_rows_recv,
    pooled_rows_send,
    pooled_rows_recv,
    mixed_rows_send,
    mixed_rows_recv,
    deep_rows_recv,
    fine_col_send,
    fine_col_recv,
    coarse_col_send,
    coarse_col_recv,
    end_send,
    end_recv,
    halo_send,
    halo_recv,
    feature_slots,
    face_slots,
    low_slots,
    high_slots,
    sum_sems,
):
    face, tile = lax.axis_index("face"), lax.axis_index("tile")
    place = (face, tile, faces, tiles)
    devices = faces * tiles
    linear = face * tiles + tile
    nbins, nch0 = fine_ref.shape[1:]
    nch1 = coarse_ref.shape[2]
    nmaps = params_ref.shape[0]
    order = fine_ref.shape[0]
    nrows = maps_ref.shape[2]
    ncols = maps_ref.shape[3] // 2
    fields = nmaps * nbins
    pooled = float(nrows // 2 * ncols * devices)

    def device_of(i):
        return (lax.div(i, tiles), lax.rem(i, tiles))

    barrier = pltpu.get_barrier_semaphore()

    def greet(k, _):
        pl.semaphore_signal(
            barrier,
            inc=1,
            device_id=device_of(lax.rem(linear + k, devices)),
            device_id_type=MESH,
        )
        return 0

    lax.fori_loop(1, devices, greet, 0)

    square = (LANES, LANES)
    ri, ci = iota(square, 0), iota(square, 1)
    even_first = onehot(ri == 2 * (ci % HALF) + ci // HALF).astype(bf16)
    flat_ref[...] = mm(maps_ref[...].reshape(-1, LANES), even_first, 1, 0, None)
    low_half = iota((fields, LANES), 1) < HALF
    zero = jnp.zeros((HALF - fields, LANES), f32)

    def row_of(r):
        return flat_ref.at[pl.ds(r, fields, stride=nrows)]

    for r in range(0, nrows, 2):
        one, two = row_of(r)[...], row_of(r + 1)[...]
        even = jnp.where(low_half, one, swap(two))
        odd = jnp.where(low_half, swap(one), two)
        both = jnp.concatenate([even, zero, odd, zero], axis=0)
        x0_ref[pl.ds(r, 2)] = both.T.reshape(2, ncols, LANES)

    pl.semaphore_wait(barrier, devices - 1)

    def exchange(i, field, rows, fine, pack, unpack):
        cols = (fine_col_send, fine_col_recv) if fine else (coarse_col_send, coarse_col_recv)
        bufs = rows + tuple(c.at[i // 2] for c in cols) + (end_send.at[i], end_recv.at[i])
        return Exchange(field, bufs, halo_send.at[i], halo_recv.at[i], place, fine, pack, unpack)

    ex0 = exchange(
        0,
        x0_ref,
        (input_rows_send, input_rows_recv),
        True,
        functools.partial(pack_input, fields),
        functools.partial(unpack_input, fields),
    )
    ex0.start()

    below = lax.rem(face + 1, faces)
    spots = (lax.rem(tile + tiles - 1, tiles), tile, lax.rem(tile + 1, tiles))
    flags_up = [jnp.where(flip_ref[face, s] == 1, 1.0, 0.0).astype(f32) for s in spots]
    flags_down = [jnp.where(flip_ref[below, s] == 1, 1.0, 0.0).astype(f32) for s in spots]

    at_bin = onehot(iota((LANES, nbins), 0) % nbins == iota((LANES, nbins), 1)).astype(bf16)
    at_ch0 = onehot(iota((nch0, LANES), 1) % nch0 == iota((nch0, LANES), 0)).astype(bf16)
    at_ch1 = onehot(iota((nch1, LANES), 1) % nch1 == iota((nch1, LANES), 0)).astype(bf16)

    def spread(left, term, right, ca):
        rows = mm(left, term, ca, 0, None)
        return mm(rows.astype(bf16), right, 1, 0, None) if right is not None else rows

    def fine_mask(k):
        return onehot(
            (ri // HALF == ci // HALF)
            & ((ri % HALF) // fields == k)
            & ((ri % fields) // nbins == (ci % HALF) // nch0)
        )

    mask0 = fine_mask(0)
    mask1 = onehot((ri % HALF) // nch0 == ci // nch1)
    w0, mixing = [], [0.0, 0.0]
    for k in range(order):
        terms = [spread(at_bin, t, at_ch0, 1) for t in split(fine_ref[k])]
        w0.append([(mask0 * t).astype(bf16) for t in terms])
        mixing = [m + fine_mask(k) * t for m, t in zip(mixing, terms)]
    mixing = [m.astype(bf16) for m in mixing]
    w1 = [
        [(mask1 * spread(at_ch0, t, at_ch1, 0)).astype(bf16) for t in split(coarse_ref[k])]
        for k in range(order)
    ]
    wf = [spread(at_ch1, t, None, 0).astype(bf16) for t in split(feature_ref[...])]
    head_mask = onehot(iota((nmaps, LANES), 0) == iota((nmaps, LANES), 1) // nch1)

    first, second = ex0.finish(flags_up, flags_down)
    t0_ref[0] = first
    t0_ref[1] = second

    def flat(x):
        return x.reshape(-1, LANES)

    def conv(terms, weights, cb):
        highs, lows = zip(*[split(flat(t)) for t in terms])
        whighs, wlows = zip(*weights)
        left = jnp.concatenate(highs + lows + highs, axis=1)
        right = jnp.concatenate(whighs + whighs + wlows, axis=cb)
        return mm(left, right, 1, cb, None)

    pre0 = conv((x0_ref[...], first, second), w0, 0)
    small = jnp.exp(-jnp.abs(pre0))
    act0 = jnp.maximum(pre0, 0.0) + jnp.log1p(small)
    sig0_ref[...] = (0.25 * jnp.where(pre0 >= 0, 1.0, small) / (1.0 + small)).reshape(
        nrows, ncols, LANES
    )
    act0 = act0.reshape(nrows // 2, 2, ncols, LANES)
    x1_ref[...] = 0.25 * (act0[:, 0] + act0[:, 1])

    ex1 = exchange(
        1, x1_ref, (pooled_rows_send, pooled_rows_recv), False, pack_pooled, unpack_pooled
    )
    ex1.start()
    first, second = ex1.finish(flags_up, flags_down)
    t1_ref[0] = first
    t1_ref[1] = second
    pre1 = conv((x1_ref[...], first, second), w1, 0)
    small = jnp.exp(-jnp.abs(pre1))
    act1 = jnp.maximum(pre1, 0.0) + jnp.log1p(small)
    feature_sum = GroupSum(feature_slots, sum_sems.at[0], linear, device_of)
    feature_sum.start(jnp.sum(act1, axis=0, keepdims=True))
    sig1 = jnp.where(pre1 >= 0, 1.0, small) / (1.0 + small)
    from_params = params_ref[:, 0:1] * param_w_ref[0:1, :]
    for i in range(1, params_ref.shape[1]):
        from_params = from_params + params_ref[:, i : i + 1] * param_w_ref[i : i + 1, :]
    features = feature_sum.finish() / pooled
    hidden = jnp.tanh(mm3(split(head_mask * features), wf) + from_params)
    logits = jnp.sum(hidden * out_w_ref[...], axis=1, keepdims=True)
    spot = iota((nmaps, nmaps), 0) == iota((nmaps, nmaps), 1)
    logits_ref[...] = jnp.sum(jnp.where(spot, logits, 0.0), axis=0, keepdims=True)
    dlogit = 1.0 / (1.0 + jnp.exp(-logits)) - labels_ref[...].astype(f32)
    dhidden = dlogit * out_w_ref[...] * (1.0 - hidden * hidden)
    dfeatures = jnp.sum(head_mask * mm3(split(dhidden), wf, 1, 1), axis=0, keepdims=True)
    dpre1 = (dfeatures / pooled) * sig1
    d1_ref[...] = dpre1.reshape(nrows // 2, ncols, LANES)

    ex2 = exchange(2, d1_ref, (None, deep_rows_recv), False, None, None)
    ex2.start()

    row, lane = iota((nch0, LANES), 0), iota((nch0, LANES), 1)
    grads = jnp.zeros((nch0, LANES), f32)
    right = split(dpre1)
    for k in range(order):
        term = x1_ref[...] if k == 0 else t1_ref[k - 1]
        full = mask1 * mm3(split(flat(term)), right, 0, 0)
        part = jnp.sum(full.reshape(-1, nch0, LANES), axis=0)
        shift = LANES // 2
        while shift >= nch1:
            part = part + pltpu.roll(part, shift, axis=1)
            shift //= 2
        grads = jnp.where(lane // nch1 == k, part, grads)

    first, second = ex2.finish(flags_up, flags_down)
    dx1 = conv((d1_ref[...], first, second), w1, 1).reshape(nrows // 2, 1, ncols, LANES)
    sig0 = sig0_ref[...].reshape(nrows // 2, 2, ncols, LANES)
    dpre0 = split(flat((dx1 * sig0).reshape(nrows, ncols, LANES)))

    d0_ref[...] = mm3(dpre0, mixing, 1, 1).reshape(nrows, ncols, LANES)
    ex3 = exchange(
        3,
        d0_ref,
        (mixed_rows_send, mixed_rows_recv),
        True,
        functools.partial(pack_mixed, fields),
        functools.partial(unpack_mixed, fields),
    )
    ex3.start()
    for k in range(order):
        term = x0_ref[...] if k == 0 else t0_ref[k - 1]
        full = mask0 * mm3(split(flat(term)), dpre0, 0, 0)
        part = full[0:fields] + full[HALF : HALF + fields]
        shift = fields // 2
        while shift >= nbins:
            part = part + pltpu.roll(part, shift, axis=0)
            shift //= 2
        shift = LANES // 2
        while shift >= nch0:
            part = part + pltpu.roll(part, shift, axis=1)
            shift //= 2
        here = (row // nbins == k) & (lane // nch0 == order * nch1 // nch0)
        grads = jnp.where(here, part, grads)

    low = low_slots.shape[0]
    tile_high, tile_low = lax.div(tile, low), lax.rem(tile, low)
    sums = [
        GroupSum(low_slots, sum_sems.at[1], tile_low, lambda j: (face, tile_high * low + j)),
        GroupSum(face_slots, sum_sems.at[2], face, lambda j: (j, tile)),
        GroupSum(high_slots, sum_sems.at[3], tile_high, lambda j: (face, j * low + tile_low)),
    ]
    sums[0].start(grads)
    def mix(x, first):
        return x + 2.0 * pltpu.roll(first, LANES - fields, axis=first.ndim - 1)

    _, outer = ex3.finish(flags_up, flags_down, mix)
    sums[1].start(sums[0].finish())
    block = lane_block((nrows, ncols, LANES), fields)
    mixed = d0_ref[...]
    pixels = float(nrows * faces * 2 * ncols * tiles)
    parts = pixels * jnp.where(block == 0, mixed, jnp.where(block == 1, outer, -mixed))
    for r in range(0, nrows, 2):
        both = parts[r : r + 2].reshape(LANES, LANES).T
        even, odd = [
            both[h : h + fields] + both[h + fields : h + 2 * fields] + both[h + 2 * fields : h + 3 * fields]
            for h in (0, HALF)
        ]
        row_of(r)[...] = jnp.where(low_half, even, swap(odd))
        row_of(r + 1)[...] = jnp.where(low_half, swap(even), odd)
    sums[2].start(sums[1].finish())
    woven = jnp.concatenate(split(flat_ref[...]), axis=1)
    twice = jnp.concatenate([even_first, even_first], axis=1)
    sal_ref[...] = mm(woven, twice, 1, 1, None).reshape(sal_ref.shape)
    grads = sums[2].finish()
    for k in range(order):
        grad_c_ref[k] = grads[:, k * nch1 : (k + 1) * nch1]
        start = order * nch1
        grad_f_ref[k] = grads[k * nbins : (k + 1) * nbins, start : start + nch0]


def on_device(faces, tiles, maps, params, labels, flip, fine_w, coarse_w, feature_w, param_w, out_w):
    nmaps, nbins, nrows, width = maps.shape
    ncols = width // 2
    low = 1
    while low * low < tiles:
        low *= 2
    vmem = pl.BlockSpec(memory_space=pltpu.VMEM)
    smem = pl.BlockSpec(memory_space=pltpu.SMEM)
    fine = (nrows, ncols, LANES)
    coarse = (nrows // 2, ncols, LANES)

    def buf(*shape):
        return pltpu.VMEM(shape, f32)

    logits, saliency, grad_f, grad_c = pl.pallas_call(
        functools.partial(kernel, faces, tiles),
        out_shape=(
            jax.ShapeDtypeStruct((1, nmaps), f32),
            jax.ShapeDtypeStruct(maps.shape, f32),
            jax.ShapeDtypeStruct(fine_w.shape, f32),
            jax.ShapeDtypeStruct(coarse_w.shape, f32),
        ),
        in_specs=[vmem, vmem, vmem, smem, vmem, vmem, vmem, vmem, vmem],
        out_specs=(vmem,) * 4,
        scratch_shapes=[
            buf(*fine),
            buf(2, *fine),
            buf(*fine),
            buf(*coarse),
            buf(2, *coarse),
            buf(*coarse),
            buf(*fine),
            buf(nmaps * nbins * nrows, width),
            buf(2, ncols // 2, LANES),
            buf(2, ncols // 2, LANES),
            buf(2, ncols, LANES),
            buf(2, ncols, LANES),
            buf(2, ncols, LANES),
            buf(2, ncols, LANES),
            buf(2, 2, ncols, LANES),
            buf(2, 2, 1, nrows, 1, LANES),
            buf(2, 2, 1, nrows, 1, LANES),
            buf(2, 2, 2, nrows // 2, 1, LANES),
            buf(2, 2, 2, nrows // 2, 1, LANES),
            buf(4, 2, 2, 1, LANES),
            buf(4, 4, 2, 1, LANES),
            pltpu.SemaphoreType.DMA((4, 8)),
            pltpu.SemaphoreType.DMA((4, 8)),
            buf(faces * tiles, 1, LANES),
            buf(faces, fine_w.shape[2], LANES),
            buf(low, fine_w.shape[2], LANES),
            buf(tiles // low, fine_w.shape[2], LANES),
            pltpu.SemaphoreType.DMA((4, 2)),
        ],
        compiler_params=pltpu.CompilerParams(
            collective_id=0, has_side_effects=True, vmem_limit_bytes=48 * 1024 * 1024
        ),
    )(
        maps,
        params,
        labels.reshape(nmaps, 1),
        flip,
        fine_w,
        coarse_w,
        feature_w,
        param_w,
        out_w.reshape(1, -1),
    )
    return logits.reshape(nmaps), saliency, grad_f, grad_c


def solution(mesh):
    in_specs = (P(None, None, "face", "tile"), P(), P(), P(), P(), P(), P(), P(), P())
    out_specs = (P(), P(None, None, "face", "tile"), P(), P())
    body = functools.partial(on_device, mesh.shape["face"], mesh.shape["tile"])
    return jax.shard_map(body, mesh=mesh, in_specs=in_specs, out_specs=out_specs, check_vma=False)
```

```python
import functools

import jax
import jax.numpy as jnp
from jax import lax
from jax.experimental import pallas as pl
from jax.experimental.pallas import tpu as pltpu
from jax.sharding import PartitionSpec as P

f32 = jnp.float32
bf16 = jnp.bfloat16
exact = lax.Precision.HIGHEST
MESH = pl.DeviceIdType.MESH
LANES = 128
HALF = 64
UP, DOWN, LEFT, RIGHT, UL, UR, DL, DR = range(8)


def mm(a, b, ca=1, cb=0, precision=exact):
    return lax.dot_general(
        a, b, (((ca,), (cb,)), ((), ())), precision=precision, preferred_element_type=f32
    )


def split(x):
    high = x.astype(bf16)
    return high, (x - high.astype(f32)).astype(bf16)


def mm3(a, b, ca=1, cb=0):
    (ah, al), (bh, bl) = a, b
    left = jnp.concatenate([ah, al, ah], axis=ca)
    right = jnp.concatenate([bh, bh, bl], axis=cb)
    return mm(left, right, ca, cb, None)


def iota(shape, dim):
    return lax.broadcasted_iota(jnp.int32, shape, dim)


def onehot(cond):
    return jnp.where(cond, 1.0, 0.0).astype(f32)


def swap(x):
    return pltpu.roll(x, HALF, axis=x.ndim - 1)


def pick(flag, yes, no):
    return flag * yes + (1.0 - flag) * no


def from_left(x, edge):
    axis = x.ndim - 2
    return jnp.where(iota(x.shape, axis) == 0, edge, pltpu.roll(x, 1, axis=axis))


def from_right(x, edge):
    axis = x.ndim - 2
    n = x.shape[axis]
    return jnp.where(iota(x.shape, axis) == n - 1, edge, pltpu.roll(x, n - 1, axis=axis))


def beside(x, left, right, fine):
    if not fine:
        return from_left(x, left) + from_right(x, right)
    s = swap(x)
    even = iota(x.shape, x.ndim - 1) < HALF
    return s + jnp.where(even, from_left(s, swap(left)), from_right(s, swap(right)))


def lap(x, up, down, left, right, fine):
    above = jnp.concatenate([up[None], x[:-1]], axis=0)
    below = jnp.concatenate([x[1:], down[None]], axis=0)
    return -0.25 * (above + below + beside(x, left, right, fine))


def lane_block(shape, size):
    return (iota(shape, len(shape) - 1) % HALF) // size


def pack_input(size, near, far):
    pair = near + pltpu.roll(far, size, axis=1)
    n = pair.shape[0] // 2
    return pair[:n] + pltpu.roll(pair[n:], 2 * size, axis=1)


def unpack_input(size, packed):
    def block(i):
        here = packed if i == 0 else pltpu.roll(packed, LANES - i * size, axis=1)
        return jnp.where(lane_block(here.shape, size) == 0, here, 0.0)

    near = jnp.concatenate([block(0), block(2)], axis=0)
    far = jnp.concatenate([block(1), block(3)], axis=0)
    return near, far


def pack_pooled(near, far):
    low = iota(near.shape, 1) < HALF
    return jnp.where(low, near + swap(near), far + swap(far))


def unpack_pooled(packed):
    low = iota(packed.shape, 1) < HALF
    return jnp.where(low, packed, 0.0), jnp.where(low, 0.0, packed)


def pack_mixed(size, near, far):
    return jnp.where(
        lane_block(near.shape, size) == 3, pltpu.roll(far, size, axis=1), near
    )


def unpack_mixed(size, packed):
    return packed, pltpu.roll(packed, LANES - size, axis=1)


class Exchange:
    def __init__(self, field, bufs, send_sem, recv_sem, place, fine, pack, unpack):
        self.field, self.place, self.fine = field, place, fine
        self.pack, self.unpack = pack, unpack
        self.row_send, self.row_recv = bufs[:2]
        self.col_send, self.col_recv, self.end_send, self.end_recv = bufs[2:]
        self.send_sem, self.recv_sem = send_sem, recv_sem

    def start(self):
        field, (face, tile, faces, tiles) = self.field, self.place
        nrows, ncols, _ = field.shape
        up, down = lax.rem(face + faces - 1, faces), lax.rem(face + 1, faces)
        left, right = lax.rem(tile + tiles - 1, tiles), lax.rem(tile + 1, tiles)
        copies = [None] * 8

        def send(way, src, dst, target):
            copies[way] = pltpu.make_async_remote_copy(
                src_ref=src,
                dst_ref=dst,
                send_sem=self.send_sem.at[way],
                recv_sem=self.recv_sem.at[way],
                device_id=target,
                device_id_type=MESH,
            )
            copies[way].start()

        if self.pack is None:
            send(UP, field.at[pl.ds(0, 2)], self.row_recv.at[1], (up, tile))
            send(DOWN, field.at[pl.ds(nrows - 2, 2)], self.row_recv.at[0], (down, tile))
        else:
            self.row_send[0] = self.pack(field[0], field[1])
            send(UP, self.row_send.at[0], self.row_recv.at[1], (up, tile))
            self.row_send[1] = self.pack(field[nrows - 1], field[nrows - 2])
            send(DOWN, self.row_send.at[1], self.row_recv.at[0], (down, tile))
        for side, row in ((0, 0), (1, nrows - 1)):
            self.end_send[side, 0] = field[row, 0:1, :]
            self.end_send[side, 1] = field[row, ncols - 1 : ncols, :]
        send(UL, self.end_send.at[0], self.end_recv.at[3], (up, left))
        send(UR, self.end_send.at[0], self.end_recv.at[2], (up, right))
        send(DL, self.end_send.at[1], self.end_recv.at[1], (down, left))
        send(DR, self.end_send.at[1], self.end_recv.at[0], (down, right))
        width = self.col_send.shape[1]
        for w in range(width):
            self.col_send[0, w] = field[:, w : w + 1, :]
            self.col_send[1, w] = field[:, ncols - 1 - w : ncols - w, :]
        send(LEFT, self.col_send.at[0], self.col_recv.at[1], (face, left))
        send(RIGHT, self.col_send.at[1], self.col_recv.at[0], (face, right))
        self.copies = copies

    def rows(self, side):
        got = self.row_recv[side]
        if self.pack is None:
            return (got[1], got[0]) if side == 0 else (got[0], got[1])
        return self.unpack(got)

    def turn(self, x):
        return swap(x) if self.fine else x

    def outer(self, flags, rows, end_left, end_right):
        flag_left, flag, flag_right = flags
        ncols = rows[0].shape[0]
        at = (ncols, 2 * ncols)
        mirror = onehot(iota(at, 0) + iota(at, 1) % ncols == ncols - 1).astype(bf16)
        pair = jnp.concatenate(split(jnp.concatenate(rows, axis=1)), axis=0)
        turned = mm(mirror, pair, 1, 0, None)
        rows = [
            pick(flag, self.turn(turned[:, LANES * i : LANES * (i + 1)]), rows[i]) for i in range(2)
        ]
        row_left = pick(flag, self.turn(end_right[0]), end_left[1])
        row_right = pick(flag, self.turn(end_left[1]), end_right[0])
        col_left = pick(flag_left, self.turn(end_left[0]), end_left[1])
        col_right = pick(flag_right, self.turn(end_right[1]), end_right[0])
        return rows, row_left, row_right, col_left, col_right

    def finish(self, flags_up, flags_down, mix=None):
        for copy in self.copies:
            copy.wait()
        fine = self.fine
        x = self.field[...]
        nrows, ncols, _ = x.shape
        ends = self.end_recv[...]
        (u1, u2), ul, ur, lu, ru = self.outer(flags_up, self.rows(0), ends[0], ends[1])
        (d1, d2), dl, dr, ld, rd = self.outer(flags_down, self.rows(1), ends[2], ends[3])
        lefts, rights = self.col_recv[0], self.col_recv[1]
        first = lap(x, u1, d1, lefts[0], rights[0], fine)
        first_u = -0.25 * (u2 + x[0] + beside(u1, ul, ur, fine))
        first_d = -0.25 * (d2 + x[nrows - 1] + beside(d1, dl, dr, fine))
        if fine:
            along_l = swap(lefts[0]) + swap(self.field[:, 0:1, :])
            along_r = swap(rights[0]) + swap(self.field[:, ncols - 1 : ncols, :])
        else:
            along_l = lefts[1] + self.field[:, 0:1, :]
            along_r = rights[1] + self.field[:, ncols - 1 : ncols, :]

        def edge(col, over, under, along):
            above = jnp.concatenate([over[None], col[:-1]], axis=0)
            below = jnp.concatenate([col[1:], under[None]], axis=0)
            return -0.25 * (above + below + along)

        first_l = edge(lefts[0], lu, ld, along_l)
        first_r = edge(rights[0], ru, rd, along_r)
        if mix is None:
            return first, 2.0 * lap(first, first_u, first_d, first_l, first_r, fine) - x
        return first, lap(
            mix(x, first),
            mix(u1, first_u),
            mix(d1, first_d),
            mix(lefts[0], first_l),
            mix(rights[0], first_r),
            fine,
        )


class GroupSum:
    def __init__(self, slots, sems, me, visit):
        self.slots, self.sems, self.me, self.visit = slots, sems, me, visit
        self.count = slots.shape[0]

    def start(self, value):
        mine = self.slots.at[self.me]
        mine[...] = value

        def send(device):
            pltpu.make_async_remote_copy(
                src_ref=mine,
                dst_ref=mine,
                send_sem=self.sems.at[0],
                recv_sem=self.sems.at[1],
                device_id=device,
                device_id_type=MESH,
            ).start()

        self.visit(send)

    def finish(self):
        others = self.slots.at[pl.ds(0, self.count - 1)]
        pltpu.make_async_copy(others, others, self.sems.at[1]).wait()
        pltpu.make_async_copy(others, others, self.sems.at[0]).wait()
        return jnp.sum(self.slots[...], axis=0)


def ring(me, count, device_of):
    def visit(act):
        for k in range(1, count):
            act(device_of(lax.rem(me + k, count)))

    return visit


def everyone(face, tile, faces, tiles):
    def row(act, f, first):
        where = face if isinstance(f, int) and f == 0 else lax.rem(face + f, faces)

        def step(t, _):
            act((where, lax.rem(tile + t, tiles)))
            return 0

        if tiles <= 16:
            for t in range(first, tiles):
                step(t, 0)
        else:
            lax.fori_loop(first, tiles, step, 0)

    def visit(act):
        row(act, 0, 1)

        def other(f, _):
            row(act, f, 0)
            return 0

        if faces <= 2:
            for f in range(1, faces):
                other(f, 0)
        else:
            lax.fori_loop(1, faces, other, 0)

    return visit


def write_kernel(*refs):
    count = len(refs) // 2
    sems = refs[-1]
    copies = [
        pltpu.make_async_copy(refs[i], refs[count + i], sems.at[i]) for i in range(count)
    ]
    for copy in copies:
        copy.start()
    for copy in copies:
        copy.wait()


def kernel(
    faces,
    tiles,
    *refs,
):
    inputs, outputs, held = refs[:9], refs[9:13], refs[13:22]
    input_sems, work = refs[22], refs[23:]
    loads = [
        pltpu.make_async_copy(inputs[i], held[i], input_sems.at[i]) for i in range(len(inputs))
    ]
    for load in loads:
        load.start()
    run(faces, tiles, loads, *held, *outputs, *work)


def run(
    faces,
    tiles,
    loads,
    maps_ref,
    params_ref,
    labels_ref,
    flip_ref,
    fine_ref,
    coarse_ref,
    feature_ref,
    param_w_ref,
    out_w_ref,
    logits_ref,
    sal_ref,
    grad_f_ref,
    grad_c_ref,
    x0_ref,
    t0_ref,
    sig0_ref,
    x1_ref,
    t1_ref,
    d1_ref,
    d0_ref,
    flat_ref,
    input_rows_send,
    input_rows_recv,
    pooled_rows_send,
    pooled_rows_recv,
    mixed_rows_send,
    mixed_rows_recv,
    deep_rows_recv,
    fine_col_send,
    fine_col_recv,
    coarse_col_send,
    coarse_col_recv,
    end_send,
    end_recv,
    halo_send,
    halo_recv,
    feature_slots,
    face_slots,
    low_slots,
    high_slots,
    sum_sems,
):
    face, tile = lax.axis_index("face"), lax.axis_index("tile")
    place = (face, tile, faces, tiles)
    devices = faces * tiles
    linear = face * tiles + tile
    nbins, nch0 = fine_ref.shape[1:]
    nch1 = coarse_ref.shape[2]
    nmaps = params_ref.shape[1]
    order = fine_ref.shape[0]
    nrows = maps_ref.shape[2]
    ncols = maps_ref.shape[3] // 2
    fields = nmaps * nbins
    pooled = float(nrows // 2 * ncols * devices)

    to_everyone = everyone(face, tile, faces, tiles)
    barrier = pltpu.get_barrier_semaphore()

    def greet(device):
        pl.semaphore_signal(barrier, inc=1, device_id=device, device_id_type=MESH)

    to_everyone(greet)

    square = (LANES, LANES)
    ri, ci = iota(square, 0), iota(square, 1)
    even_first = onehot(ri == 2 * (ci % HALF) + ci // HALF).astype(bf16)
    loads[0].wait()
    flat_ref[...] = mm(maps_ref[...].reshape(-1, LANES), even_first, 1, 0, None)
    low_half = iota((fields, LANES), 1) < HALF
    zero = jnp.zeros((HALF - fields, LANES), f32)

    def row_of(r):
        return flat_ref.at[pl.ds(r, fields, stride=nrows)]

    for r in range(0, nrows, 2):
        one, two = row_of(r)[...], row_of(r + 1)[...]
        even = jnp.where(low_half, one, swap(two))
        odd = jnp.where(low_half, swap(one), two)
        both = jnp.concatenate([even, zero, odd, zero], axis=0)
        x0_ref[pl.ds(r, 2)] = both.T.reshape(2, ncols, LANES)

    pl.semaphore_wait(barrier, devices - 1)

    def exchange(i, field, rows, fine, pack, unpack):
        cols = (fine_col_send, fine_col_recv) if fine else (coarse_col_send, coarse_col_recv)
        bufs = rows + tuple(c.at[i // 2] for c in cols) + (end_send.at[i], end_recv.at[i])
        return Exchange(field, bufs, halo_send.at[i], halo_recv.at[i], place, fine, pack, unpack)

    ex0 = exchange(
        0,
        x0_ref,
        (input_rows_send, input_rows_recv),
        True,
        functools.partial(pack_input, fields),
        functools.partial(unpack_input, fields),
    )
    ex0.start()
    for load in loads[1:]:
        load.wait()

    below = lax.rem(face + 1, faces)
    spots = (lax.rem(tile + tiles - 1, tiles), tile, lax.rem(tile + 1, tiles))
    flags_up = [jnp.where(flip_ref[face, s] == 1, 1.0, 0.0).astype(f32) for s in spots]
    flags_down = [jnp.where(flip_ref[below, s] == 1, 1.0, 0.0).astype(f32) for s in spots]

    at_bin = onehot(iota((LANES, nbins), 0) % nbins == iota((LANES, nbins), 1)).astype(bf16)
    at_ch0 = onehot(iota((nch0, LANES), 1) % nch0 == iota((nch0, LANES), 0)).astype(bf16)
    at_ch1 = onehot(iota((nch1, LANES), 1) % nch1 == iota((nch1, LANES), 0)).astype(bf16)

    def spread(left, term, right, ca):
        rows = mm(left, term, ca, 0, None)
        return mm(rows.astype(bf16), right, 1, 0, None) if right is not None else rows

    def fine_mask(k):
        return onehot(
            (ri // HALF == ci // HALF)
            & ((ri % HALF) // fields == k)
            & ((ri % fields) // nbins == (ci % HALF) // nch0)
        )

    mask0 = fine_mask(0)
    mask1 = onehot((ri % HALF) // nch0 == ci // nch1)
    w0, mixing = [], [0.0, 0.0]
    for k in range(order):
        terms = [spread(at_bin, t, at_ch0, 1) for t in split(fine_ref[k])]
        w0.append([(mask0 * t).astype(bf16) for t in terms])
        mixing = [m + fine_mask(k) * t for m, t in zip(mixing, terms)]
    mixing = [m.astype(bf16) for m in mixing]
    w1 = [
        [(mask1 * spread(at_ch0, t, at_ch1, 0)).astype(bf16) for t in split(coarse_ref[k])]
        for k in range(order)
    ]
    wf = [spread(at_ch1, t, None, 0).astype(bf16) for t in split(feature_ref[...])]
    head_mask = onehot(iota((nmaps, LANES), 0) == iota((nmaps, LANES), 1) // nch1)
    from_params = mm(params_ref[...], param_w_ref[...], 0, 0)
    spot = iota((nmaps, nmaps), 0) == iota((nmaps, nmaps), 1)
    labels = jnp.sum(
        jnp.where(spot, labels_ref[...].astype(f32), 0.0), axis=1, keepdims=True
    )

    first, second = ex0.finish(flags_up, flags_down)
    t0_ref[0] = first
    t0_ref[1] = second

    def flat(x):
        return x.reshape(-1, LANES)

    def conv(terms, weights, cb):
        highs, lows = zip(*[split(flat(t)) for t in terms])
        whighs, wlows = zip(*weights)
        left = jnp.concatenate(highs + lows + highs, axis=1)
        right = jnp.concatenate(whighs + whighs + wlows, axis=cb)
        return mm(left, right, 1, cb, None)

    pre0 = conv((x0_ref[...], first, second), w0, 0)
    small = jnp.exp(-jnp.abs(pre0))
    act0 = jnp.maximum(pre0, 0.0) + jnp.log1p(small)
    sig0_ref[...] = (0.25 * jnp.where(pre0 >= 0, 1.0, small) / (1.0 + small)).reshape(
        nrows, ncols, LANES
    )
    act0 = act0.reshape(nrows // 2, 2, ncols, LANES)
    x1_ref[...] = 0.25 * (act0[:, 0] + act0[:, 1])

    ex1 = exchange(
        1, x1_ref, (pooled_rows_send, pooled_rows_recv), False, pack_pooled, unpack_pooled
    )
    ex1.start()
    first, second = ex1.finish(flags_up, flags_down)
    t1_ref[0] = first
    t1_ref[1] = second
    pre1 = conv((x1_ref[...], first, second), w1, 0)
    small = jnp.exp(-jnp.abs(pre1))
    act1 = jnp.maximum(pre1, 0.0) + jnp.log1p(small)
    feature_sum = GroupSum(feature_slots, sum_sems.at[0], linear, to_everyone)
    feature_sum.start(jnp.sum(act1, axis=0, keepdims=True))

    sig1 = jnp.where(pre1 >= 0, 1.0, small) / (1.0 + small)
    d1_ref[...] = sig1.reshape(nrows // 2, ncols, LANES)
    ex2 = exchange(2, d1_ref, (None, deep_rows_recv), False, None, None)
    ex2.start()

    row, lane = iota((nch0, LANES), 0), iota((nch0, LANES), 1)
    unscaled = []
    right = split(sig1)
    for k in range(order):
        term = x1_ref[...] if k == 0 else t1_ref[k - 1]
        full = mask1 * mm3(split(flat(term)), right, 0, 0)
        unscaled.append(jnp.sum(full.reshape(-1, nch0, LANES), axis=0))

    features = feature_sum.finish() / pooled
    hidden = jnp.tanh(mm3(split(head_mask * features), wf) + from_params)
    logits = jnp.sum(hidden * out_w_ref[...], axis=1, keepdims=True)
    logits_ref[...] = jnp.sum(jnp.where(spot, logits, 0.0), axis=0, keepdims=True)
    dlogit = 1.0 / (1.0 + jnp.exp(-logits)) - labels
    dhidden = dlogit * out_w_ref[...] * (1.0 - hidden * hidden)
    dfeatures = jnp.sum(head_mask * mm3(split(dhidden), wf, 1, 1), axis=0, keepdims=True)
    scale = dfeatures / pooled
    scaled = [split(scale * (h.astype(f32) + l.astype(f32))) for h, l in w1]

    first, second = ex2.finish(flags_up, flags_down)
    dx1 = conv((d1_ref[...], first, second), scaled, 1).reshape(nrows // 2, 1, ncols, LANES)
    sig0 = sig0_ref[...].reshape(nrows // 2, 2, ncols, LANES)
    dpre0 = split(flat((dx1 * sig0).reshape(nrows, ncols, LANES)))

    d0_ref[...] = mm3(dpre0, mixing, 1, 1).reshape(nrows, ncols, LANES)
    ex3 = exchange(
        3,
        d0_ref,
        (mixed_rows_send, mixed_rows_recv),
        True,
        functools.partial(pack_mixed, fields),
        functools.partial(unpack_mixed, fields),
    )
    ex3.start()
    grads = jnp.zeros((nch0, LANES), f32)
    for k in range(order):
        part = scale * unscaled[k]
        shift = LANES // 2
        while shift >= nch1:
            part = part + pltpu.roll(part, shift, axis=1)
            shift //= 2
        grads = jnp.where(lane // nch1 == k, part, grads)
    for k in range(order):
        term = x0_ref[...] if k == 0 else t0_ref[k - 1]
        full = mask0 * mm3(split(flat(term)), dpre0, 0, 0)
        part = full[0:fields] + full[HALF : HALF + fields]
        shift = fields // 2
        while shift >= nbins:
            part = part + pltpu.roll(part, shift, axis=0)
            shift //= 2
        shift = LANES // 2
        while shift >= nch0:
            part = part + pltpu.roll(part, shift, axis=1)
            shift //= 2
        here = (row // nbins == k) & (lane // nch0 == order * nch1 // nch0)
        grads = jnp.where(here, part, grads)

    low = low_slots.shape[0]
    tile_high, tile_low = lax.div(tile, low), lax.rem(tile, low)
    groups = (
        (low_slots, tile_low, lambda j: (face, tile_high * low + j)),
        (face_slots, face, lambda j: (j, tile)),
        (high_slots, tile_high, lambda j: (face, j * low + tile_low)),
    )
    sums = [
        GroupSum(slots, sum_sems.at[1 + i], me, ring(me, slots.shape[0], device_of))
        for i, (slots, me, device_of) in enumerate(groups)
    ]
    sums[0].start(grads)
    def mix(x, first):
        return x + 2.0 * pltpu.roll(first, LANES - fields, axis=first.ndim - 1)

    _, outer = ex3.finish(flags_up, flags_down, mix)
    sums[1].start(sums[0].finish())
    block = lane_block((nrows, ncols, LANES), fields)
    mixed = d0_ref[...]
    pixels = float(nrows * faces * 2 * ncols * tiles)
    parts = pixels * jnp.where(block == 0, mixed, jnp.where(block == 1, outer, -mixed))
    for r in range(0, nrows, 2):
        both = parts[r : r + 2].reshape(LANES, LANES).T
        even, odd = [
            both[h : h + fields] + both[h + fields : h + 2 * fields] + both[h + 2 * fields : h + 3 * fields]
            for h in (0, HALF)
        ]
        row_of(r)[...] = jnp.where(low_half, even, swap(odd))
        row_of(r + 1)[...] = jnp.where(low_half, swap(even), odd)
    sums[2].start(sums[1].finish())
    woven = jnp.concatenate(split(flat_ref[...]), axis=1)
    twice = jnp.concatenate([even_first, even_first], axis=1)
    sal_ref[...] = mm(woven, twice, 1, 1, None).reshape(sal_ref.shape)
    grads = sums[2].finish()
    for k in range(order):
        grad_c_ref[k] = grads[:, k * nch1 : (k + 1) * nch1]
        start = order * nch1
        grad_f_ref[k] = grads[k * nbins : (k + 1) * nbins, start : start + nch0]


def on_device(faces, tiles, maps, params, labels, flip, fine_w, coarse_w, feature_w, param_w, out_w):
    nmaps, nbins, nrows, width = maps.shape
    ncols = width // 2
    low = 1
    while low * low < tiles:
        low *= 2
    vmem = pl.BlockSpec(memory_space=pltpu.VMEM)
    fine = (nrows, ncols, LANES)
    coarse = (nrows // 2, ncols, LANES)

    def buf(*shape):
        return pltpu.VMEM(shape, f32)

    operands = (
        maps,
        params.T,
        labels.reshape(1, nmaps),
        flip,
        fine_w,
        coarse_w,
        feature_w,
        param_w,
        out_w.reshape(1, -1),
    )
    held = [pltpu.VMEM(x.shape, x.dtype) for x in operands]
    held[3] = pltpu.SMEM(flip.shape, flip.dtype)
    anywhere = pl.BlockSpec(memory_space=pl.ANY)
    results = pl.pallas_call(
        functools.partial(kernel, faces, tiles),
        out_shape=(
            jax.ShapeDtypeStruct((1, nmaps), f32),
            jax.ShapeDtypeStruct(maps.shape, f32),
            jax.ShapeDtypeStruct(fine_w.shape, f32),
            jax.ShapeDtypeStruct(coarse_w.shape, f32),
        ),
        in_specs=[anywhere] * len(operands),
        out_specs=(vmem,) * 4,
        scratch_shapes=[
            *held,
            pltpu.SemaphoreType.DMA((len(operands),)),
            buf(*fine),
            buf(2, *fine),
            buf(*fine),
            buf(*coarse),
            buf(2, *coarse),
            buf(*coarse),
            buf(*fine),
            buf(nmaps * nbins * nrows, width),
            buf(2, ncols // 2, LANES),
            buf(2, ncols // 2, LANES),
            buf(2, ncols, LANES),
            buf(2, ncols, LANES),
            buf(2, ncols, LANES),
            buf(2, ncols, LANES),
            buf(2, 2, ncols, LANES),
            buf(2, 2, 1, nrows, 1, LANES),
            buf(2, 2, 1, nrows, 1, LANES),
            buf(2, 2, 2, nrows // 2, 1, LANES),
            buf(2, 2, 2, nrows // 2, 1, LANES),
            buf(4, 2, 2, 1, LANES),
            buf(4, 4, 2, 1, LANES),
            pltpu.SemaphoreType.DMA((4, 8)),
            pltpu.SemaphoreType.DMA((4, 8)),
            buf(faces * tiles, 1, LANES),
            buf(faces, fine_w.shape[2], LANES),
            buf(low, fine_w.shape[2], LANES),
            buf(tiles // low, fine_w.shape[2], LANES),
            pltpu.SemaphoreType.DMA((4, 2)),
        ],
        compiler_params=pltpu.CompilerParams(
            collective_id=0, has_side_effects=True, vmem_limit_bytes=60 * 1024 * 1024
        ),
    )(*operands)
    logits, saliency, grad_f, grad_c = pl.pallas_call(
        write_kernel,
        out_shape=tuple(jax.ShapeDtypeStruct(x.shape, x.dtype) for x in results),
        in_specs=[anywhere] * len(results),
        out_specs=(anywhere,) * len(results),
        scratch_shapes=[pltpu.SemaphoreType.DMA((len(results),))],
        compiler_params=pltpu.CompilerParams(vmem_limit_bytes=60 * 1024 * 1024),
    )(*results)
    return logits.reshape(nmaps), saliency, grad_f, grad_c


def solution(mesh):
    in_specs = (P(None, None, "face", "tile"), P(), P(), P(), P(), P(), P(), P(), P())
    out_specs = (P(), P(None, None, "face", "tile"), P(), P())
    body = functools.partial(on_device, mesh.shape["face"], mesh.shape["tile"])
    return jax.shard_map(body, mesh=mesh, in_specs=in_specs, out_specs=out_specs, check_vma=False)
```

```python
import functools

import jax
import jax.numpy as jnp
from jax import lax
from jax.experimental import pallas as pl
from jax.experimental.pallas import tpu as pltpu
from jax.sharding import PartitionSpec as P

f32 = jnp.float32
bf16 = jnp.bfloat16
exact = lax.Precision.HIGHEST
MESH = pl.DeviceIdType.MESH
LANES = 128
HALF = 64
UP, DOWN, LEFT, RIGHT, UL, UR, DL, DR = range(8)


def mm(a, b, ca=1, cb=0, precision=exact):
    return lax.dot_general(
        a, b, (((ca,), (cb,)), ((), ())), precision=precision, preferred_element_type=f32
    )


def split(x):
    high = x.astype(bf16)
    return high, (x - high.astype(f32)).astype(bf16)


def mm3(a, b, ca=1, cb=0):
    (ah, al), (bh, bl) = a, b
    left = jnp.concatenate([ah, al, ah], axis=ca)
    right = jnp.concatenate([bh, bh, bl], axis=cb)
    return mm(left, right, ca, cb, None)


def iota(shape, dim):
    return lax.broadcasted_iota(jnp.int32, shape, dim)


def onehot(cond):
    return jnp.where(cond, 1.0, 0.0).astype(f32)


def swap(x):
    return pltpu.roll(x, HALF, axis=x.ndim - 1)


def pick(flag, yes, no):
    return flag * yes + (1.0 - flag) * no


def from_left(x, edge):
    axis = x.ndim - 2
    return jnp.where(iota(x.shape, axis) == 0, edge, pltpu.roll(x, 1, axis=axis))


def from_right(x, edge):
    axis = x.ndim - 2
    n = x.shape[axis]
    return jnp.where(iota(x.shape, axis) == n - 1, edge, pltpu.roll(x, n - 1, axis=axis))


def beside(x, left, right, fine):
    if not fine:
        return from_left(x, left) + from_right(x, right)
    s = swap(x)
    even = iota(x.shape, x.ndim - 1) < HALF
    return s + jnp.where(even, from_left(s, swap(left)), from_right(s, swap(right)))


def lap_row(ref, r, up, down, left, right, fine):
    above = up if r == 0 else ref[r - 1]
    below = down if r == ref.shape[0] - 1 else ref[r + 1]
    return -0.25 * (above + below + beside(ref[r], left, right, fine))


def lane_block(shape, size):
    return (iota(shape, len(shape) - 1) % HALF) // size


def pack_input(size, near, far):
    pair = near + pltpu.roll(far, size, axis=1)
    n = pair.shape[0] // 2
    return pair[:n] + pltpu.roll(pair[n:], 2 * size, axis=1)


def unpack_input(size, packed):
    def block(i):
        here = packed if i == 0 else pltpu.roll(packed, LANES - i * size, axis=1)
        return jnp.where(lane_block(here.shape, size) == 0, here, 0.0)

    near = jnp.concatenate([block(0), block(2)], axis=0)
    far = jnp.concatenate([block(1), block(3)], axis=0)
    return near, far


def pack_pooled(near, far):
    low = iota(near.shape, 1) < HALF
    return jnp.where(low, near + swap(near), far + swap(far))


def unpack_pooled(packed):
    low = iota(packed.shape, 1) < HALF
    return jnp.where(low, packed, 0.0), jnp.where(low, 0.0, packed)


def pack_mixed(size, near, far):
    return jnp.where(
        lane_block(near.shape, size) == 3, pltpu.roll(far, size, axis=1), near
    )


def unpack_mixed(size, packed):
    return packed, pltpu.roll(packed, LANES - size, axis=1)


class Exchange:
    def __init__(self, field, bufs, send_sem, recv_sem, place, fine, pack, unpack):
        self.field, self.place, self.fine = field, place, fine
        self.pack, self.unpack = pack, unpack
        self.row_send, self.row_recv = bufs[:2]
        self.col_send, self.col_recv, self.end_send, self.end_recv = bufs[2:]
        self.send_sem, self.recv_sem = send_sem, recv_sem

    def start(self):
        field, (face, tile, faces, tiles) = self.field, self.place
        nrows, ncols, _ = field.shape
        up, down = lax.rem(face + faces - 1, faces), lax.rem(face + 1, faces)
        left, right = lax.rem(tile + tiles - 1, tiles), lax.rem(tile + 1, tiles)
        copies = [None] * 8

        def send(way, src, dst, target):
            copies[way] = pltpu.make_async_remote_copy(
                src_ref=src,
                dst_ref=dst,
                send_sem=self.send_sem.at[way],
                recv_sem=self.recv_sem.at[way],
                device_id=target,
                device_id_type=MESH,
            )
            copies[way].start()

        if self.pack is None:
            send(UP, field.at[pl.ds(0, 2)], self.row_recv.at[1], (up, tile))
            send(DOWN, field.at[pl.ds(nrows - 2, 2)], self.row_recv.at[0], (down, tile))
        else:
            self.row_send[0] = self.pack(field[0], field[1])
            send(UP, self.row_send.at[0], self.row_recv.at[1], (up, tile))
            self.row_send[1] = self.pack(field[nrows - 1], field[nrows - 2])
            send(DOWN, self.row_send.at[1], self.row_recv.at[0], (down, tile))
        for side, row in ((0, 0), (1, nrows - 1)):
            self.end_send[side, 0] = field[row, 0:1, :]
            self.end_send[side, 1] = field[row, ncols - 1 : ncols, :]
        send(UL, self.end_send.at[0], self.end_recv.at[3], (up, left))
        send(UR, self.end_send.at[0], self.end_recv.at[2], (up, right))
        send(DL, self.end_send.at[1], self.end_recv.at[1], (down, left))
        send(DR, self.end_send.at[1], self.end_recv.at[0], (down, right))
        width = self.col_send.shape[1]
        for w in range(width):
            self.col_send[0, w] = field[:, w : w + 1, :]
            self.col_send[1, w] = field[:, ncols - 1 - w : ncols - w, :]
        send(LEFT, self.col_send.at[0], self.col_recv.at[1], (face, left))
        send(RIGHT, self.col_send.at[1], self.col_recv.at[0], (face, right))
        self.copies = copies

    def rows(self, side):
        got = self.row_recv[side]
        if self.pack is None:
            return (got[1], got[0]) if side == 0 else (got[0], got[1])
        return self.unpack(got)

    def turn(self, x):
        return swap(x) if self.fine else x

    def outer(self, flags, rows, end_left, end_right):
        flag_left, flag, flag_right = flags
        ncols = rows[0].shape[0]
        at = (ncols, 2 * ncols)
        mirror = onehot(iota(at, 0) + iota(at, 1) % ncols == ncols - 1).astype(bf16)
        pair = jnp.concatenate(split(jnp.concatenate(rows, axis=1)), axis=0)
        turned = mm(mirror, pair, 1, 0, None)
        rows = [
            pick(flag, self.turn(turned[:, LANES * i : LANES * (i + 1)]), rows[i]) for i in range(2)
        ]
        row_left = pick(flag, self.turn(end_right[0]), end_left[1])
        row_right = pick(flag, self.turn(end_left[1]), end_right[0])
        col_left = pick(flag_left, self.turn(end_left[0]), end_left[1])
        col_right = pick(flag_right, self.turn(end_right[1]), end_right[0])
        return rows, row_left, row_right, col_left, col_right

    def finish(self, flags_up, flags_down, first_ref, emit, mix=None):
        for copy in self.copies:
            copy.wait()
        fine, x = self.fine, self.field
        nrows, ncols, _ = x.shape
        ends = self.end_recv[...]
        (u1, u2), ul, ur, lu, ru = self.outer(flags_up, self.rows(0), ends[0], ends[1])
        (d1, d2), dl, dr, ld, rd = self.outer(flags_down, self.rows(1), ends[2], ends[3])
        lefts, rights = self.col_recv[0], self.col_recv[1]

        def through(x, first):
            return first if mix is None else mix(x, first)

        for r in range(nrows):
            first = lap_row(x, r, u1, d1, lefts[0, r], rights[0, r], fine)
            first_ref[r] = through(x[r], first)
        first_u = through(u1, -0.25 * (u2 + x[0] + beside(u1, ul, ur, fine)))
        first_d = through(d1, -0.25 * (d2 + x[nrows - 1] + beside(d1, dl, dr, fine)))
        if fine:
            along_l = swap(lefts[0]) + swap(x[:, 0:1, :])
            along_r = swap(rights[0]) + swap(x[:, ncols - 1 : ncols, :])
        else:
            along_l = lefts[1] + x[:, 0:1, :]
            along_r = rights[1] + x[:, ncols - 1 : ncols, :]

        def edge(col, over, under, along):
            above = jnp.concatenate([over[None], col[:-1]], axis=0)
            below = jnp.concatenate([col[1:], under[None]], axis=0)
            return through(col, -0.25 * (above + below + along))

        first_l = edge(lefts[0], lu, ld, along_l)
        first_r = edge(rights[0], ru, rd, along_r)
        for r in range(nrows):
            second = lap_row(first_ref, r, first_u, first_d, first_l[r], first_r[r], fine)
            emit(r, x[r], first_ref[r], second)


class GroupSum:
    def __init__(self, slots, sems, me, visit):
        self.slots, self.sems, self.me, self.visit = slots, sems, me, visit
        self.count = slots.shape[0]

    def start(self, value):
        mine = self.slots.at[self.me]
        mine[...] = value

        def send(device):
            pltpu.make_async_remote_copy(
                src_ref=mine,
                dst_ref=mine,
                send_sem=self.sems.at[0],
                recv_sem=self.sems.at[1],
                device_id=device,
                device_id_type=MESH,
            ).start()

        self.visit(send)

    def finish(self):
        others = self.slots.at[pl.ds(0, self.count - 1)]
        pltpu.make_async_copy(others, others, self.sems.at[1]).wait()
        pltpu.make_async_copy(others, others, self.sems.at[0]).wait()
        return jnp.sum(self.slots[...], axis=0)


def ring(me, count, device_of):
    def visit(act):
        for k in range(1, count):
            act(device_of(lax.rem(me + k, count)))

    return visit


def everyone(face, tile, faces, tiles):
    def row(act, f, first):
        where = face if isinstance(f, int) and f == 0 else lax.rem(face + f, faces)

        def step(t, _):
            act((where, lax.rem(tile + t, tiles)))
            return 0

        if tiles <= 16:
            for t in range(first, tiles):
                step(t, 0)
        else:
            lax.fori_loop(first, tiles, step, 0)

    def visit(act):
        row(act, 0, 1)

        def other(f, _):
            row(act, f, 0)
            return 0

        if faces <= 2:
            for f in range(1, faces):
                other(f, 0)
        else:
            lax.fori_loop(1, faces, other, 0)

    return visit


def write_kernel(*refs):
    count = len(refs) // 3
    sources, targets, held, sems = refs[:count], refs[count : 2 * count], refs[2 * count : -1], refs[-1]
    loads = [pltpu.make_async_copy(sources[i], held[i], sems.at[0, i]) for i in range(count)]
    stores = [pltpu.make_async_copy(held[i], targets[i], sems.at[1, i]) for i in range(count)]
    for load in loads:
        load.start()
    for load, store in zip(loads, stores):
        load.wait()
        store.start()
    for store in stores:
        store.wait()


def kernel(
    faces,
    tiles,
    *refs,
):
    inputs, outputs, held, made = refs[:9], refs[9:13], refs[13:22], refs[22:26]
    input_sems, output_sems, work = refs[26], refs[27], refs[28:]
    loads = [
        pltpu.make_async_copy(inputs[i], held[i], input_sems.at[i]) for i in range(len(inputs))
    ]
    for load in loads:
        load.start()
    stores = [
        pltpu.make_async_copy(made[i], outputs[i], output_sems.at[i]) for i in range(len(outputs))
    ]
    run(faces, tiles, loads, stores, *held, *made, *work)
    for store in stores:
        store.wait()


def run(
    faces,
    tiles,
    loads,
    stores,
    maps_ref,
    params_ref,
    labels_ref,
    flip_ref,
    fine_ref,
    coarse_ref,
    feature_ref,
    param_w_ref,
    out_w_ref,
    logits_ref,
    sal_ref,
    grad_f_ref,
    grad_c_ref,
    x0_ref,
    first0_ref,
    split0_ref,
    pre0_ref,
    sig0_ref,
    x1_ref,
    first1_ref,
    split1_ref,
    d1_ref,
    split_d1_ref,
    d0_ref,
    split_d0_ref,
    flat_ref,
    input_rows_send,
    input_rows_recv,
    pooled_rows_send,
    pooled_rows_recv,
    mixed_rows_send,
    mixed_rows_recv,
    deep_rows_recv,
    fine_col_send,
    fine_col_recv,
    coarse_col_send,
    coarse_col_recv,
    end_send,
    end_recv,
    halo_send,
    halo_recv,
    feature_slots,
    face_slots,
    low_slots,
    high_slots,
    sum_sems,
):
    face, tile = lax.axis_index("face"), lax.axis_index("tile")
    place = (face, tile, faces, tiles)
    devices = faces * tiles
    linear = face * tiles + tile
    nbins, nch0 = fine_ref.shape[1:]
    nch1 = coarse_ref.shape[2]
    nmaps = params_ref.shape[1]
    order = fine_ref.shape[0]
    nrows = maps_ref.shape[2]
    ncols = maps_ref.shape[3] // 2
    fields = nmaps * nbins
    pooled = float(nrows // 2 * ncols * devices)

    to_everyone = everyone(face, tile, faces, tiles)
    barrier = pltpu.get_barrier_semaphore()

    def greet(device):
        pl.semaphore_signal(barrier, inc=1, device_id=device, device_id_type=MESH)

    to_everyone(greet)

    square = (LANES, LANES)
    ri, ci = iota(square, 0), iota(square, 1)
    even_first = onehot(ri == 2 * (ci % HALF) + ci // HALF).astype(bf16)
    loads[0].wait()
    flat_ref[...] = mm(maps_ref[...].reshape(-1, LANES), even_first, 1, 0, None)
    low_half = iota((fields, LANES), 1) < HALF
    zero = jnp.zeros((HALF - fields, LANES), f32)

    def row_of(r):
        return flat_ref.at[pl.ds(r, fields, stride=nrows)]

    for r in range(0, nrows, 2):
        one, two = row_of(r)[...], row_of(r + 1)[...]
        even = jnp.where(low_half, one, swap(two))
        odd = jnp.where(low_half, swap(one), two)
        both = jnp.concatenate([even, zero, odd, zero], axis=0)
        x0_ref[pl.ds(r, 2)] = both.T.reshape(2, ncols, LANES)

    pl.semaphore_wait(barrier, devices - 1)

    def exchange(i, field, rows, fine, pack, unpack):
        cols = (fine_col_send, fine_col_recv) if fine else (coarse_col_send, coarse_col_recv)
        bufs = rows + tuple(c.at[i // 2] for c in cols) + (end_send.at[i], end_recv.at[i])
        return Exchange(field, bufs, halo_send.at[i], halo_recv.at[i], place, fine, pack, unpack)

    ex0 = exchange(
        0,
        x0_ref,
        (input_rows_send, input_rows_recv),
        True,
        functools.partial(pack_input, fields),
        functools.partial(unpack_input, fields),
    )
    ex0.start()
    for load in loads[1:]:
        load.wait()

    below = lax.rem(face + 1, faces)
    spots = (lax.rem(tile + tiles - 1, tiles), tile, lax.rem(tile + 1, tiles))
    flags_up = [jnp.where(flip_ref[face, s] == 1, 1.0, 0.0).astype(f32) for s in spots]
    flags_down = [jnp.where(flip_ref[below, s] == 1, 1.0, 0.0).astype(f32) for s in spots]

    at_bin = onehot(iota((LANES, nbins), 0) % nbins == iota((LANES, nbins), 1)).astype(bf16)
    at_ch0 = onehot(iota((nch0, LANES), 1) % nch0 == iota((nch0, LANES), 0)).astype(bf16)
    at_ch1 = onehot(iota((nch1, LANES), 1) % nch1 == iota((nch1, LANES), 0)).astype(bf16)

    def spread(left, term, right, ca):
        rows = mm(left, term, ca, 0, None)
        return mm(rows.astype(bf16), right, 1, 0, None) if right is not None else rows

    def fine_mask(k):
        return onehot(
            (ri // HALF == ci // HALF)
            & ((ri % HALF) // fields == k)
            & ((ri % fields) // nbins == (ci % HALF) // nch0)
        )

    mask0 = [fine_mask(k) for k in range(order)]
    mask1 = onehot((ri % HALF) // nch0 == ci // nch1)
    mixing = [0.0, 0.0]
    for k in range(order):
        terms = [spread(at_bin, t, at_ch0, 1) for t in split(fine_ref[k])]
        mixing = [m + mask0[k] * t for m, t in zip(mixing, terms)]
    mixing = [m.astype(bf16) for m in mixing]
    w1 = [
        [(mask1 * spread(at_ch0, t, at_ch1, 0)).astype(bf16) for t in split(coarse_ref[k])]
        for k in range(order)
    ]
    wf = [spread(at_ch1, t, None, 0).astype(bf16) for t in split(feature_ref[...])]
    head_mask = onehot(iota((nmaps, LANES), 0) == iota((nmaps, LANES), 1) // nch1)
    from_params = mm(params_ref[...], param_w_ref[...], 0, 0)
    spot = iota((nmaps, nmaps), 0) == iota((nmaps, nmaps), 1)
    labels = jnp.sum(
        jnp.where(spot, labels_ref[...].astype(f32), 0.0), axis=1, keepdims=True
    )

    def beside_lows(weights, axis):
        highs, lows = [jnp.concatenate(w, axis=axis) for w in zip(*weights)]
        return jnp.concatenate(
            [
                jnp.concatenate([highs, highs], axis=axis),
                jnp.concatenate([lows, jnp.zeros_like(lows)], axis=axis),
            ],
            axis=1 - axis,
        )

    def folded(x):
        return x[:, :LANES] + x[:, LANES:]

    def put(ref, r, places, x):
        for place, part in zip(places, split(x)):
            ref[r * ncols : (r + 1) * ncols, place * LANES : (place + 1) * LANES] = part

    def soft(v):
        small = jnp.exp(-jnp.abs(v))
        sig = jnp.where(v >= 0, 1.0, small) / (1.0 + small)
        return jnp.maximum(v, 0.0) + jnp.log1p(small), sig

    mix_forward, mix_back = beside_lows([mixing], 0), beside_lows([mixing], 1)

    def emit_fine(r, x, first, outer):
        second = 2.0 * outer - x
        terms = x + pltpu.roll(first, fields, axis=1) + pltpu.roll(second, 2 * fields, axis=1)
        put(split0_ref, r, (0, 1), terms)

    ex0.finish(flags_up, flags_down, first0_ref, emit_fine)
    pre0_ref[...] = folded(mm(split0_ref[...], mix_forward, 1, 0, None)).reshape(pre0_ref.shape)
    for r in range(0, nrows, 2):
        acts = []
        for q in (r, r + 1):
            act, sig = soft(pre0_ref[q])
            sig0_ref[q] = 0.25 * sig
            acts.append(act)
        x1_ref[r // 2] = 0.25 * (acts[0] + acts[1])

    ex1 = exchange(
        1, x1_ref, (pooled_rows_send, pooled_rows_recv), False, pack_pooled, unpack_pooled
    )
    ex1.start()
    coarse_forward = beside_lows(w1, 0)

    def emit_coarse(r, x, first, outer):
        for k, term in enumerate((x, first, 2.0 * outer - x)):
            put(split1_ref, r, (k, order + k), term)

    ex1.finish(flags_up, flags_down, first1_ref, emit_coarse)
    pre1 = folded(mm(split1_ref[...], coarse_forward, 1, 0, None))
    act_sum = jnp.zeros((ncols, LANES), f32)
    for r in range(nrows // 2):
        act, sig = soft(pre1[r * ncols : (r + 1) * ncols])
        act_sum = act_sum + act
        d1_ref[r] = sig
    feature_sum = GroupSum(feature_slots, sum_sems.at[0], linear, to_everyone)
    feature_sum.start(jnp.sum(act_sum, axis=0, keepdims=True))

    ex2 = exchange(2, d1_ref, (None, deep_rows_recv), False, None, None)
    ex2.start()

    row, lane = iota((nch0, LANES), 0), iota((nch0, LANES), 1)
    for r in range(nrows // 2):
        put(split_d1_ref, r, (0, 1), d1_ref[r])
    products = mm(split1_ref[...], split_d1_ref[...], 0, 0, None)
    unscaled = []
    for k in range(order):
        full = folded(products[k * LANES : (k + 1) * LANES])
        full = full + products[(order + k) * LANES : (order + k + 1) * LANES, :LANES]
        unscaled.append(jnp.sum((mask1 * full).reshape(-1, nch0, LANES), axis=0))

    features = feature_sum.finish() / pooled
    hidden = jnp.tanh(mm3(split(head_mask * features), wf) + from_params)
    logits = jnp.sum(hidden * out_w_ref[...], axis=1, keepdims=True)
    logits_ref[...] = jnp.sum(jnp.where(spot, logits, 0.0), axis=0, keepdims=True)
    stores[0].start()
    dlogit = 1.0 / (1.0 + jnp.exp(-logits)) - labels
    dhidden = dlogit * out_w_ref[...] * (1.0 - hidden * hidden)
    dfeatures = jnp.sum(head_mask * mm3(split(dhidden), wf, 1, 1), axis=0, keepdims=True)
    scale = dfeatures / pooled
    scaled = [split(scale * (h.astype(f32) + l.astype(f32))) for h, l in w1]

    coarse_back = beside_lows(scaled, 1)
    ex2.finish(flags_up, flags_down, first1_ref, emit_coarse)
    dx1 = folded(mm(split1_ref[...], coarse_back, 1, 1, None))
    for r in range(nrows):
        put(split_d0_ref, r, (0, 1), dx1[r // 2 * ncols : (r // 2 + 1) * ncols] * sig0_ref[r])

    d0_ref[...] = folded(mm(split_d0_ref[...], mix_back, 1, 1, None)).reshape(d0_ref.shape)
    ex3 = exchange(
        3,
        d0_ref,
        (mixed_rows_send, mixed_rows_recv),
        True,
        functools.partial(pack_mixed, fields),
        functools.partial(unpack_mixed, fields),
    )
    ex3.start()
    grads = jnp.zeros((nch0, LANES), f32)
    for k in range(order):
        part = scale * unscaled[k]
        shift = LANES // 2
        while shift >= nch1:
            part = part + pltpu.roll(part, shift, axis=1)
            shift //= 2
        grads = jnp.where(lane // nch1 == k, part, grads)
    products = mm(split0_ref[...], split_d0_ref[...], 0, 0, None)
    products = folded(products[:LANES]) + products[LANES:, :LANES]
    for k in range(order):
        full = mask0[k] * products
        start = k * fields
        part = full[start : start + fields] + full[HALF + start : HALF + start + fields]
        shift = fields // 2
        while shift >= nbins:
            part = part + pltpu.roll(part, shift, axis=0)
            shift //= 2
        shift = LANES // 2
        while shift >= nch0:
            part = part + pltpu.roll(part, shift, axis=1)
            shift //= 2
        here = (row // nbins == k) & (lane // nch0 == order * nch1 // nch0)
        grads = jnp.where(here, part, grads)

    low = low_slots.shape[0]
    tile_high, tile_low = lax.div(tile, low), lax.rem(tile, low)
    groups = (
        (low_slots, tile_low, lambda j: (face, tile_high * low + j)),
        (face_slots, face, lambda j: (j, tile)),
        (high_slots, tile_high, lambda j: (face, j * low + tile_low)),
    )
    sums = [
        GroupSum(slots, sum_sems.at[1 + i], me, ring(me, slots.shape[0], device_of))
        for i, (slots, me, device_of) in enumerate(groups)
    ]
    sums[0].start(grads)
    def mix(x, first):
        return x + 2.0 * pltpu.roll(first, LANES - fields, axis=first.ndim - 1)

    block = lane_block((ncols, LANES), fields)
    pixels = float(nrows * faces * 2 * ncols * tiles)

    def emit_back(r, x, first, outer):
        sig0_ref[r] = pixels * jnp.where(block == 0, x, jnp.where(block == 1, outer, -x))

    ex3.finish(flags_up, flags_down, first0_ref, emit_back, mix)
    sums[1].start(sums[0].finish())
    for r in range(0, nrows, 2):
        both = sig0_ref[pl.ds(r, 2)].reshape(LANES, LANES).T
        even, odd = [
            both[h : h + fields] + both[h + fields : h + 2 * fields] + both[h + 2 * fields : h + 3 * fields]
            for h in (0, HALF)
        ]
        row_of(r)[...] = jnp.where(low_half, even, swap(odd))
        row_of(r + 1)[...] = jnp.where(low_half, swap(even), odd)
    sums[2].start(sums[1].finish())
    woven = jnp.concatenate(split(flat_ref[...]), axis=1)
    twice = jnp.concatenate([even_first, even_first], axis=1)
    sal_ref[...] = mm(woven, twice, 1, 1, None).reshape(sal_ref.shape)
    stores[1].start()
    grads = sums[2].finish()
    for k in range(order):
        grad_c_ref[k] = grads[:, k * nch1 : (k + 1) * nch1]
        start = order * nch1
        grad_f_ref[k] = grads[k * nbins : (k + 1) * nbins, start : start + nch0]
    stores[2].start()
    stores[3].start()


def on_device(faces, tiles, maps, params, labels, flip, fine_w, coarse_w, feature_w, param_w, out_w):
    nmaps, nbins, nrows, width = maps.shape
    ncols = width // 2
    low = 1
    while low * low < tiles:
        low *= 2
    fine = (nrows, ncols, LANES)
    coarse = (nrows // 2, ncols, LANES)

    def buf(*shape):
        return pltpu.VMEM(shape, f32)

    operands = (
        maps,
        params.T,
        labels.reshape(1, nmaps),
        flip,
        fine_w,
        coarse_w,
        feature_w,
        param_w,
        out_w.reshape(1, -1),
    )
    held = [pltpu.VMEM(x.shape, x.dtype) for x in operands]
    held[3] = pltpu.SMEM(flip.shape, flip.dtype)
    anywhere = pl.BlockSpec(memory_space=pl.ANY)
    shapes = ((1, nmaps), maps.shape, fine_w.shape, coarse_w.shape)
    results = pl.pallas_call(
        functools.partial(kernel, faces, tiles),
        out_shape=tuple(jax.ShapeDtypeStruct(shape, f32) for shape in shapes),
        in_specs=[anywhere] * len(operands),
        out_specs=(anywhere,) * 4,
        scratch_shapes=[
            *held,
            *[buf(*shape) for shape in shapes],
            pltpu.SemaphoreType.DMA((len(operands),)),
            pltpu.SemaphoreType.DMA((len(shapes),)),
            buf(*fine),
            buf(*fine),
            pltpu.VMEM((nrows * ncols, 2 * LANES), bf16),
            buf(*fine),
            buf(*fine),
            buf(*coarse),
            buf(*coarse),
            pltpu.VMEM((nrows // 2 * ncols, 2 * fine_w.shape[0] * LANES), bf16),
            buf(*coarse),
            pltpu.VMEM((nrows // 2 * ncols, 2 * LANES), bf16),
            buf(*fine),
            pltpu.VMEM((nrows * ncols, 2 * LANES), bf16),
            buf(nmaps * nbins * nrows, width),
            buf(2, ncols // 2, LANES),
            buf(2, ncols // 2, LANES),
            buf(2, ncols, LANES),
            buf(2, ncols, LANES),
            buf(2, ncols, LANES),
            buf(2, ncols, LANES),
            buf(2, 2, ncols, LANES),
            buf(2, 2, 1, nrows, 1, LANES),
            buf(2, 2, 1, nrows, 1, LANES),
            buf(2, 2, 2, nrows // 2, 1, LANES),
            buf(2, 2, 2, nrows // 2, 1, LANES),
            buf(4, 2, 2, 1, LANES),
            buf(4, 4, 2, 1, LANES),
            pltpu.SemaphoreType.DMA((4, 8)),
            pltpu.SemaphoreType.DMA((4, 8)),
            buf(faces * tiles, 1, LANES),
            buf(faces, fine_w.shape[2], LANES),
            buf(low, fine_w.shape[2], LANES),
            buf(tiles // low, fine_w.shape[2], LANES),
            pltpu.SemaphoreType.DMA((4, 2)),
        ],
        compiler_params=pltpu.CompilerParams(
            collective_id=0, has_side_effects=True, vmem_limit_bytes=60 * 1024 * 1024
        ),
    )(*operands)
    logits, saliency, grad_f, grad_c = pl.pallas_call(
        write_kernel,
        out_shape=tuple(jax.ShapeDtypeStruct(x.shape, x.dtype) for x in results),
        in_specs=[anywhere] * len(results),
        out_specs=(anywhere,) * len(results),
        scratch_shapes=[
            *[pltpu.VMEM(x.shape, x.dtype) for x in results],
            pltpu.SemaphoreType.DMA((2, len(results))),
        ],
        compiler_params=pltpu.CompilerParams(vmem_limit_bytes=60 * 1024 * 1024),
    )(*results)
    return logits.reshape(nmaps), saliency, grad_f, grad_c


def solution(mesh):
    in_specs = (P(None, None, "face", "tile"), P(), P(), P(), P(), P(), P(), P(), P())
    out_specs = (P(), P(None, None, "face", "tile"), P(), P())
    body = functools.partial(on_device, mesh.shape["face"], mesh.shape["tile"])
    return jax.shard_map(body, mesh=mesh, in_specs=in_specs, out_specs=out_specs, check_vma=False)
```

```python
import functools

import jax
import jax.numpy as jnp
from jax import lax
from jax.experimental import pallas as pl
from jax.experimental.pallas import tpu as pltpu
from jax.sharding import PartitionSpec as P

f32 = jnp.float32
bf16 = jnp.bfloat16
exact = lax.Precision.HIGHEST
MESH = pl.DeviceIdType.MESH
LANES = 128
HALF = 64
UP, DOWN, LEFT, RIGHT, UL, UR, DL, DR = range(8)


def mm(a, b, ca=1, cb=0, precision=exact):
    return lax.dot_general(
        a, b, (((ca,), (cb,)), ((), ())), precision=precision, preferred_element_type=f32
    )


def split(x):
    high = x.astype(bf16)
    return high, (x - high.astype(f32)).astype(bf16)


def mm3(a, b, ca=1, cb=0):
    (ah, al), (bh, bl) = a, b
    left = jnp.concatenate([ah, al, ah], axis=ca)
    right = jnp.concatenate([bh, bh, bl], axis=cb)
    return mm(left, right, ca, cb, None)


def iota(shape, dim):
    return lax.broadcasted_iota(jnp.int32, shape, dim)


def onehot(cond):
    return jnp.where(cond, 1.0, 0.0).astype(f32)


def swap(x):
    return pltpu.roll(x, HALF, axis=x.ndim - 1)


def pick(flag, yes, no):
    return flag * yes + (1.0 - flag) * no


def from_left(x, edge):
    axis = x.ndim - 2
    return jnp.where(iota(x.shape, axis) == 0, edge, pltpu.roll(x, 1, axis=axis))


def from_right(x, edge):
    axis = x.ndim - 2
    n = x.shape[axis]
    return jnp.where(iota(x.shape, axis) == n - 1, edge, pltpu.roll(x, n - 1, axis=axis))


def beside(x, left, right, fine):
    if not fine:
        return from_left(x, left) + from_right(x, right)
    s = swap(x)
    even = iota(x.shape, x.ndim - 1) < HALF
    return s + jnp.where(even, from_left(s, swap(left)), from_right(s, swap(right)))


def lap_row(ref, r, up, down, left, right, fine):
    above = up if r == 0 else ref[r - 1]
    below = down if r == ref.shape[0] - 1 else ref[r + 1]
    return -0.25 * (above + below + beside(ref[r], left, right, fine))


def lane_block(shape, size):
    return (iota(shape, len(shape) - 1) % HALF) // size


def pack_input(size, near, far):
    pair = near + pltpu.roll(far, size, axis=1)
    n = pair.shape[0] // 2
    return pair[:n] + pltpu.roll(pair[n:], 2 * size, axis=1)


def unpack_input(size, packed):
    def block(i):
        here = packed if i == 0 else pltpu.roll(packed, LANES - i * size, axis=1)
        return jnp.where(lane_block(here.shape, size) == 0, here, 0.0)

    near = jnp.concatenate([block(0), block(2)], axis=0)
    far = jnp.concatenate([block(1), block(3)], axis=0)
    return near, far


def pack_pooled(near, far):
    low = iota(near.shape, 1) < HALF
    return jnp.where(low, near + swap(near), far + swap(far))


def unpack_pooled(packed):
    low = iota(packed.shape, 1) < HALF
    return jnp.where(low, packed, 0.0), jnp.where(low, 0.0, packed)


def pack_mixed(size, near, far):
    return jnp.where(
        lane_block(near.shape, size) == 3, pltpu.roll(far, size, axis=1), near
    )


def unpack_mixed(size, packed):
    return packed, pltpu.roll(packed, LANES - size, axis=1)


class Exchange:
    def __init__(self, field, bufs, send_sem, recv_sem, place, fine, pack, unpack):
        self.field, self.place, self.fine = field, place, fine
        self.pack, self.unpack = pack, unpack
        self.row_send, self.row_recv = bufs[:2]
        self.col_send, self.col_recv, self.end_send, self.end_recv = bufs[2:]
        self.send_sem, self.recv_sem = send_sem, recv_sem

    def start(self):
        field, (face, tile, faces, tiles) = self.field, self.place
        nrows, ncols, _ = field.shape
        up, down = lax.rem(face + faces - 1, faces), lax.rem(face + 1, faces)
        left, right = lax.rem(tile + tiles - 1, tiles), lax.rem(tile + 1, tiles)
        copies = [None] * 8

        def send(way, src, dst, target):
            copies[way] = pltpu.make_async_remote_copy(
                src_ref=src,
                dst_ref=dst,
                send_sem=self.send_sem.at[way],
                recv_sem=self.recv_sem.at[way],
                device_id=target,
                device_id_type=MESH,
            )
            copies[way].start()

        if self.pack is None:
            send(UP, field.at[pl.ds(0, 2)], self.row_recv.at[1], (up, tile))
            send(DOWN, field.at[pl.ds(nrows - 2, 2)], self.row_recv.at[0], (down, tile))
        else:
            self.row_send[0] = self.pack(field[0], field[1])
            send(UP, self.row_send.at[0], self.row_recv.at[1], (up, tile))
            self.row_send[1] = self.pack(field[nrows - 1], field[nrows - 2])
            send(DOWN, self.row_send.at[1], self.row_recv.at[0], (down, tile))
        for side, row in ((0, 0), (1, nrows - 1)):
            self.end_send[side, 0] = field[row, 0:1, :]
            self.end_send[side, 1] = field[row, ncols - 1 : ncols, :]
        send(UL, self.end_send.at[0], self.end_recv.at[3], (up, left))
        send(UR, self.end_send.at[0], self.end_recv.at[2], (up, right))
        send(DL, self.end_send.at[1], self.end_recv.at[1], (down, left))
        send(DR, self.end_send.at[1], self.end_recv.at[0], (down, right))
        width = self.col_send.shape[1]
        for w in range(width):
            self.col_send[0, w] = field[:, w : w + 1, :]
            self.col_send[1, w] = field[:, ncols - 1 - w : ncols - w, :]
        send(LEFT, self.col_send.at[0], self.col_recv.at[1], (face, left))
        send(RIGHT, self.col_send.at[1], self.col_recv.at[0], (face, right))
        self.copies = copies

    def rows(self, side):
        got = self.row_recv[side]
        if self.pack is None:
            return (got[1], got[0]) if side == 0 else (got[0], got[1])
        return self.unpack(got)

    def turn(self, x):
        return swap(x) if self.fine else x

    def outer(self, flags, rows, end_left, end_right):
        flag_left, flag, flag_right = flags
        ncols = rows[0].shape[0]
        at = (ncols, 2 * ncols)
        mirror = onehot(iota(at, 0) + iota(at, 1) % ncols == ncols - 1).astype(bf16)
        pair = jnp.concatenate(split(jnp.concatenate(rows, axis=1)), axis=0)
        turned = mm(mirror, pair, 1, 0, None)
        rows = [
            pick(flag, self.turn(turned[:, LANES * i : LANES * (i + 1)]), rows[i]) for i in range(2)
        ]
        row_left = pick(flag, self.turn(end_right[0]), end_left[1])
        row_right = pick(flag, self.turn(end_left[1]), end_right[0])
        col_left = pick(flag_left, self.turn(end_left[0]), end_left[1])
        col_right = pick(flag_right, self.turn(end_right[1]), end_right[0])
        return rows, row_left, row_right, col_left, col_right

    def finish(self, flags_up, flags_down, first_ref, emit, mix=None):
        for copy in self.copies:
            copy.wait()
        fine, x = self.fine, self.field
        nrows, ncols, _ = x.shape
        ends = self.end_recv[...]
        (u1, u2), ul, ur, lu, ru = self.outer(flags_up, self.rows(0), ends[0], ends[1])
        (d1, d2), dl, dr, ld, rd = self.outer(flags_down, self.rows(1), ends[2], ends[3])
        lefts, rights = self.col_recv[0], self.col_recv[1]

        def through(x, first):
            return first if mix is None else mix(x, first)

        for r in range(nrows):
            first = lap_row(x, r, u1, d1, lefts[0, r], rights[0, r], fine)
            first_ref[r] = through(x[r], first)
        first_u = through(u1, -0.25 * (u2 + x[0] + beside(u1, ul, ur, fine)))
        first_d = through(d1, -0.25 * (d2 + x[nrows - 1] + beside(d1, dl, dr, fine)))
        if fine:
            along_l = swap(lefts[0]) + swap(x[:, 0:1, :])
            along_r = swap(rights[0]) + swap(x[:, ncols - 1 : ncols, :])
        else:
            along_l = lefts[1] + x[:, 0:1, :]
            along_r = rights[1] + x[:, ncols - 1 : ncols, :]

        def edge(col, over, under, along):
            above = jnp.concatenate([over[None], col[:-1]], axis=0)
            below = jnp.concatenate([col[1:], under[None]], axis=0)
            return through(col, -0.25 * (above + below + along))

        first_l = edge(lefts[0], lu, ld, along_l)
        first_r = edge(rights[0], ru, rd, along_r)
        for r in range(nrows):
            second = lap_row(first_ref, r, first_u, first_d, first_l[r], first_r[r], fine)
            emit(r, x[r], first_ref[r], second)


class GroupSum:
    def __init__(self, slots, sems, me, visit):
        self.slots, self.sems, self.me, self.visit = slots, sems, me, visit
        self.count = slots.shape[0]

    def start(self, value):
        mine = self.slots.at[self.me]
        mine[...] = value

        def send(device):
            pltpu.make_async_remote_copy(
                src_ref=mine,
                dst_ref=mine,
                send_sem=self.sems.at[0],
                recv_sem=self.sems.at[1],
                device_id=device,
                device_id_type=MESH,
            ).start()

        self.visit(send)

    def finish(self):
        others = self.slots.at[pl.ds(0, self.count - 1)]
        pltpu.make_async_copy(others, others, self.sems.at[1]).wait()
        pltpu.make_async_copy(others, others, self.sems.at[0]).wait()
        return jnp.sum(self.slots[...], axis=0)


def ring(me, count, device_of):
    def visit(act):
        def step(k, _):
            act(device_of(lax.rem(me + k, count)))
            return 0

        if count <= 8:
            for k in range(1, count):
                step(k, 0)
        else:
            lax.fori_loop(1, count, step, 0)

    return visit


def everyone(face, tile, faces, tiles):
    def row(act, f, first):
        where = face if isinstance(f, int) and f == 0 else lax.rem(face + f, faces)

        def step(t, _):
            act((where, lax.rem(tile + t, tiles)))
            return 0

        if tiles <= 16:
            for t in range(first, tiles):
                step(t, 0)
        else:
            lax.fori_loop(first, tiles, step, 0)

    def visit(act):
        row(act, 0, 1)

        def other(f, _):
            row(act, f, 0)
            return 0

        if faces <= 2:
            for f in range(1, faces):
                other(f, 0)
        else:
            lax.fori_loop(1, faces, other, 0)

    return visit


def write_kernel(*refs):
    count = len(refs) // 3
    sources, targets, held, sems = refs[:count], refs[count : 2 * count], refs[2 * count : -1], refs[-1]
    loads = [pltpu.make_async_copy(sources[i], held[i], sems.at[0, i]) for i in range(count)]
    stores = [pltpu.make_async_copy(held[i], targets[i], sems.at[1, i]) for i in range(count)]
    for load in loads:
        load.start()
    for load, store in zip(loads, stores):
        load.wait()
        store.start()
    for store in stores:
        store.wait()


def kernel(
    faces,
    tiles,
    *refs,
):
    inputs, outputs, held, made = refs[:9], refs[9:13], refs[13:22], refs[22:26]
    input_sems, output_sems, work = refs[26], refs[27], refs[28:]
    loads = [
        pltpu.make_async_copy(inputs[i], held[i], input_sems.at[i]) for i in range(len(inputs))
    ]
    for load in loads:
        load.start()
    stores = [
        pltpu.make_async_copy(made[i], outputs[i], output_sems.at[i]) for i in range(len(outputs))
    ]
    run(faces, tiles, loads, stores, *held, *made, *work)
    for store in stores:
        store.wait()


def run(
    faces,
    tiles,
    loads,
    stores,
    maps_ref,
    params_ref,
    labels_ref,
    flip_ref,
    fine_ref,
    coarse_ref,
    feature_ref,
    param_w_ref,
    out_w_ref,
    logits_ref,
    sal_ref,
    grad_f_ref,
    grad_c_ref,
    x0_ref,
    first0_ref,
    split0_ref,
    pre0_ref,
    sig0_ref,
    x1_ref,
    first1_ref,
    split1_ref,
    d1_ref,
    split_d1_ref,
    d0_ref,
    split_d0_ref,
    flat_ref,
    input_rows_send,
    input_rows_recv,
    pooled_rows_send,
    pooled_rows_recv,
    mixed_rows_send,
    mixed_rows_recv,
    deep_rows_recv,
    fine_col_send,
    fine_col_recv,
    coarse_col_send,
    coarse_col_recv,
    end_send,
    end_recv,
    halo_send,
    halo_recv,
    feature_slots,
    near_slots,
    high_slots,
    sum_sems,
):
    face, tile = lax.axis_index("face"), lax.axis_index("tile")
    place = (face, tile, faces, tiles)
    devices = faces * tiles
    linear = face * tiles + tile
    nbins, nch0 = fine_ref.shape[1:]
    nch1 = coarse_ref.shape[2]
    nmaps = params_ref.shape[1]
    order = fine_ref.shape[0]
    nrows = maps_ref.shape[2]
    ncols = maps_ref.shape[3] // 2
    fields = nmaps * nbins
    pooled = float(nrows // 2 * ncols * devices)

    to_everyone = everyone(face, tile, faces, tiles)
    barrier = pltpu.get_barrier_semaphore()

    def greet(device):
        pl.semaphore_signal(barrier, inc=1, device_id=device, device_id_type=MESH)

    to_everyone(greet)

    square = (LANES, LANES)
    ri, ci = iota(square, 0), iota(square, 1)
    even_first = onehot(ri == 2 * (ci % HALF) + ci // HALF).astype(bf16)
    loads[0].wait()
    flat_ref[...] = mm(maps_ref[...].reshape(-1, LANES), even_first, 1, 0, None)
    low_half = iota((fields, LANES), 1) < HALF
    zero = jnp.zeros((HALF - fields, LANES), f32)

    def row_of(r):
        return flat_ref.at[pl.ds(r, fields, stride=nrows)]

    for r in range(0, nrows, 2):
        one, two = row_of(r)[...], row_of(r + 1)[...]
        even = jnp.where(low_half, one, swap(two))
        odd = jnp.where(low_half, swap(one), two)
        both = jnp.concatenate([even, zero, odd, zero], axis=0)
        x0_ref[pl.ds(r, 2)] = both.T.reshape(2, ncols, LANES)

    pl.semaphore_wait(barrier, devices - 1)

    def exchange(i, field, rows, fine, pack, unpack):
        cols = (fine_col_send, fine_col_recv) if fine else (coarse_col_send, coarse_col_recv)
        bufs = rows + tuple(c.at[i // 2] for c in cols) + (end_send.at[i], end_recv.at[i])
        return Exchange(field, bufs, halo_send.at[i], halo_recv.at[i], place, fine, pack, unpack)

    ex0 = exchange(
        0,
        x0_ref,
        (input_rows_send, input_rows_recv),
        True,
        functools.partial(pack_input, fields),
        functools.partial(unpack_input, fields),
    )
    ex0.start()
    for load in loads[1:]:
        load.wait()

    below = lax.rem(face + 1, faces)
    spots = (lax.rem(tile + tiles - 1, tiles), tile, lax.rem(tile + 1, tiles))
    flags_up = [jnp.where(flip_ref[face, s] == 1, 1.0, 0.0).astype(f32) for s in spots]
    flags_down = [jnp.where(flip_ref[below, s] == 1, 1.0, 0.0).astype(f32) for s in spots]

    at_ch0 = onehot(iota((nch0, LANES), 1) % nch0 == iota((nch0, LANES), 0)).astype(bf16)
    at_ch1 = onehot(iota((nch1, LANES), 1) % nch1 == iota((nch1, LANES), 0)).astype(bf16)

    def spread(left, terms, right, ca):
        width = terms[0].shape[1]
        rows = mm(left, jnp.concatenate(terms, axis=1), ca, 0, None).astype(bf16)
        rows = [rows[:, i * width : (i + 1) * width] for i in range(len(terms))]
        if right is None:
            return rows
        full = mm(jnp.concatenate(rows, axis=0), right, 1, 0, None)
        return [full[i * LANES : (i + 1) * LANES] for i in range(len(terms))]

    mask0 = onehot(
        (ri // HALF == ci // HALF)
        & ((ri % HALF) // fields < order)
        & ((ri % fields) // nbins == (ci % HALF) // nch0)
    )
    rf, cf = iota((LANES, order * nbins), 0), iota((LANES, order * nbins), 1)
    at_term = onehot(((rf % HALF) // fields == cf // nbins) & (rf % nbins == cf % nbins))
    fine_w = jnp.concatenate([fine_ref[k] for k in range(order)], axis=0)
    mixing = spread(at_term.astype(bf16), split(fine_w), at_ch0, 1)
    mixing = [(mask0 * m).astype(bf16) for m in mixing]
    head_mask = onehot(iota((nmaps, LANES), 0) == iota((nmaps, LANES), 1) // nch1)
    from_params = mm(params_ref[...], param_w_ref[...], 0, 0)
    spot = iota((nmaps, nmaps), 0) == iota((nmaps, nmaps), 1)
    labels = jnp.sum(
        jnp.where(spot, labels_ref[...].astype(f32), 0.0), axis=1, keepdims=True
    )

    def beside_lows(weights, axis):
        highs, lows = [jnp.concatenate(w, axis=axis) for w in zip(*weights)]
        return jnp.concatenate(
            [
                jnp.concatenate([highs, highs], axis=axis),
                jnp.concatenate([lows, jnp.zeros_like(lows)], axis=axis),
            ],
            axis=1 - axis,
        )

    def folded(x):
        return x[:, :LANES] + x[:, LANES:]

    def put(ref, r, places, x):
        for place, part in zip(places, split(x)):
            ref[r * ncols : (r + 1) * ncols, place * LANES : (place + 1) * LANES] = part

    def soft(v):
        small = jnp.exp(-jnp.abs(v))
        sig = jnp.where(v >= 0, 1.0, small) / (1.0 + small)
        return jnp.maximum(v, 0.0) + jnp.log1p(small), sig

    mix_forward, mix_back = beside_lows([mixing], 0), beside_lows([mixing], 1)

    def emit_fine(r, x, first, outer):
        second = 2.0 * outer - x
        terms = x + pltpu.roll(first, fields, axis=1) + pltpu.roll(second, 2 * fields, axis=1)
        put(split0_ref, r, (0, 1), terms)

    ex0.finish(flags_up, flags_down, first0_ref, emit_fine)
    pre0_ref[...] = folded(mm(split0_ref[...], mix_forward, 1, 0, None)).reshape(pre0_ref.shape)
    for r in range(0, nrows, 2):
        acts = []
        for q in (r, r + 1):
            act, sig = soft(pre0_ref[q])
            sig0_ref[q] = 0.25 * sig
            acts.append(act)
        x1_ref[r // 2] = 0.25 * (acts[0] + acts[1])

    ex1 = exchange(
        1, x1_ref, (pooled_rows_send, pooled_rows_recv), False, pack_pooled, unpack_pooled
    )
    ex1.start()
    mask1 = onehot((ri % HALF) // nch0 == ci // nch1)
    terms = [t for k in range(order) for t in split(coarse_ref[k])]
    terms = [(mask1 * t).astype(bf16) for t in spread(at_ch0, terms, at_ch1, 0)]
    w1 = [terms[2 * k : 2 * k + 2] for k in range(order)]
    wf = spread(at_ch1, split(feature_ref[...]), None, 0)
    coarse_forward = beside_lows(w1, 0)

    def emit_coarse(r, x, first, outer):
        for k, term in enumerate((x, first, 2.0 * outer - x)):
            put(split1_ref, r, (k, order + k), term)

    ex1.finish(flags_up, flags_down, first1_ref, emit_coarse)
    pre1 = folded(mm(split1_ref[...], coarse_forward, 1, 0, None))
    act_sum = jnp.zeros((ncols, LANES), f32)
    for r in range(nrows // 2):
        act, sig = soft(pre1[r * ncols : (r + 1) * ncols])
        act_sum = act_sum + act
        d1_ref[r] = sig
    feature_sum = GroupSum(feature_slots, sum_sems.at[0], linear, to_everyone)
    feature_sum.start(jnp.sum(act_sum, axis=0, keepdims=True))

    ex2 = exchange(2, d1_ref, (None, deep_rows_recv), False, None, None)
    ex2.start()

    row, lane = iota((nch0, LANES), 0), iota((nch0, LANES), 1)
    for r in range(nrows // 2):
        put(split_d1_ref, r, (0, 1), d1_ref[r])
    products = mm(split1_ref[...], split_d1_ref[...], 0, 0, None)
    unscaled = []
    for k in range(order):
        full = folded(products[k * LANES : (k + 1) * LANES])
        full = full + products[(order + k) * LANES : (order + k + 1) * LANES, :LANES]
        unscaled.append(jnp.sum((mask1 * full).reshape(-1, nch0, LANES), axis=0))

    features = feature_sum.finish() / pooled
    hidden = jnp.tanh(mm3(split(head_mask * features), wf) + from_params)
    logits = jnp.sum(hidden * out_w_ref[...], axis=1, keepdims=True)
    logits_ref[...] = jnp.sum(jnp.where(spot, logits, 0.0), axis=0, keepdims=True)
    stores[0].start()
    dlogit = 1.0 / (1.0 + jnp.exp(-logits)) - labels
    dhidden = dlogit * out_w_ref[...] * (1.0 - hidden * hidden)
    dfeatures = jnp.sum(head_mask * mm3(split(dhidden), wf, 1, 1), axis=0, keepdims=True)
    scale = dfeatures / pooled
    scaled = [split(scale * (h.astype(f32) + l.astype(f32))) for h, l in w1]

    coarse_back = beside_lows(scaled, 1)
    ex2.finish(flags_up, flags_down, first1_ref, emit_coarse)
    dx1 = folded(mm(split1_ref[...], coarse_back, 1, 1, None))
    for r in range(nrows):
        put(split_d0_ref, r, (0, 1), dx1[r // 2 * ncols : (r // 2 + 1) * ncols] * sig0_ref[r])

    d0_ref[...] = folded(mm(split_d0_ref[...], mix_back, 1, 1, None)).reshape(d0_ref.shape)
    ex3 = exchange(
        3,
        d0_ref,
        (mixed_rows_send, mixed_rows_recv),
        True,
        functools.partial(pack_mixed, fields),
        functools.partial(unpack_mixed, fields),
    )
    ex3.start()
    grads = jnp.zeros((nch0, LANES), f32)
    for k in range(order):
        part = scale * unscaled[k]
        shift = LANES // 2
        while shift >= nch1:
            part = part + pltpu.roll(part, shift, axis=1)
            shift //= 2
        grads = jnp.where(lane // nch1 == k, part, grads)
    products = mm(split0_ref[...], split_d0_ref[...], 0, 0, None)
    full = mask0 * (folded(products[:LANES]) + products[LANES:, :LANES])
    for k in range(order):
        start = k * fields
        part = full[start : start + fields] + full[HALF + start : HALF + start + fields]
        shift = fields // 2
        while shift >= nbins:
            part = part + pltpu.roll(part, shift, axis=0)
            shift //= 2
        shift = LANES // 2
        while shift >= nch0:
            part = part + pltpu.roll(part, shift, axis=1)
            shift //= 2
        here = (row // nbins == k) & (lane // nch0 == order * nch1 // nch0)
        grads = jnp.where(here, part, grads)

    low = tiles // high_slots.shape[0]
    tile_high, tile_low = lax.div(tile, low), lax.rem(tile, low)
    my_near = face * low + tile_low

    def near_device(j):
        return lax.div(j, low), tile_high * low + lax.rem(j, low)

    groups = (
        (near_slots, my_near, near_device),
        (high_slots, tile_high, lambda j: (face, j * low + tile_low)),
    )
    sums = [
        GroupSum(slots, sum_sems.at[1 + i], me, ring(me, slots.shape[0], device_of))
        for i, (slots, me, device_of) in enumerate(groups)
    ]
    sums[0].start(grads)
    def mix(x, first):
        return x + 2.0 * pltpu.roll(first, LANES - fields, axis=first.ndim - 1)

    block = lane_block((ncols, LANES), fields)
    pixels = float(nrows * faces * 2 * ncols * tiles)

    def emit_back(r, x, first, outer):
        sig0_ref[r] = pixels * jnp.where(block == 0, x, jnp.where(block == 1, outer, -x))

    sums[1].start(sums[0].finish())
    ex3.finish(flags_up, flags_down, first0_ref, emit_back, mix)
    for r in range(0, nrows, 2):
        both = sig0_ref[pl.ds(r, 2)].reshape(LANES, LANES).T
        even, odd = [
            both[h : h + fields] + both[h + fields : h + 2 * fields] + both[h + 2 * fields : h + 3 * fields]
            for h in (0, HALF)
        ]
        row_of(r)[...] = jnp.where(low_half, even, swap(odd))
        row_of(r + 1)[...] = jnp.where(low_half, swap(even), odd)
    woven = jnp.concatenate(split(flat_ref[...]), axis=1)
    twice = jnp.concatenate([even_first, even_first], axis=1)
    sal_ref[...] = mm(woven, twice, 1, 1, None).reshape(sal_ref.shape)
    stores[1].start()
    grads = sums[1].finish()
    for k in range(order):
        grad_c_ref[k] = grads[:, k * nch1 : (k + 1) * nch1]
        start = order * nch1
        grad_f_ref[k] = grads[k * nbins : (k + 1) * nbins, start : start + nch0]
    stores[2].start()
    stores[3].start()


def on_device(faces, tiles, maps, params, labels, flip, fine_w, coarse_w, feature_w, param_w, out_w):
    nmaps, nbins, nrows, width = maps.shape
    ncols = width // 2
    low = 1
    while low * low < tiles:
        low *= 2
    fine = (nrows, ncols, LANES)
    coarse = (nrows // 2, ncols, LANES)

    def buf(*shape):
        return pltpu.VMEM(shape, f32)

    operands = (
        maps,
        params.T,
        labels.reshape(1, nmaps),
        flip,
        fine_w,
        coarse_w,
        feature_w,
        param_w,
        out_w.reshape(1, -1),
    )
    held = [pltpu.VMEM(x.shape, x.dtype) for x in operands]
    held[3] = pltpu.SMEM(flip.shape, flip.dtype)
    anywhere = pl.BlockSpec(memory_space=pl.ANY)
    shapes = ((1, nmaps), maps.shape, fine_w.shape, coarse_w.shape)
    results = pl.pallas_call(
        functools.partial(kernel, faces, tiles),
        out_shape=tuple(jax.ShapeDtypeStruct(shape, f32) for shape in shapes),
        in_specs=[anywhere] * len(operands),
        out_specs=(anywhere,) * 4,
        scratch_shapes=[
            *held,
            *[buf(*shape) for shape in shapes],
            pltpu.SemaphoreType.DMA((len(operands),)),
            pltpu.SemaphoreType.DMA((len(shapes),)),
            buf(*fine),
            buf(*fine),
            pltpu.VMEM((nrows * ncols, 2 * LANES), bf16),
            buf(*fine),
            buf(*fine),
            buf(*coarse),
            buf(*coarse),
            pltpu.VMEM((nrows // 2 * ncols, 2 * fine_w.shape[0] * LANES), bf16),
            buf(*coarse),
            pltpu.VMEM((nrows // 2 * ncols, 2 * LANES), bf16),
            buf(*fine),
            pltpu.VMEM((nrows * ncols, 2 * LANES), bf16),
            buf(nmaps * nbins * nrows, width),
            buf(2, ncols // 2, LANES),
            buf(2, ncols // 2, LANES),
            buf(2, ncols, LANES),
            buf(2, ncols, LANES),
            buf(2, ncols, LANES),
            buf(2, ncols, LANES),
            buf(2, 2, ncols, LANES),
            buf(2, 2, 1, nrows, 1, LANES),
            buf(2, 2, 1, nrows, 1, LANES),
            buf(2, 2, 2, nrows // 2, 1, LANES),
            buf(2, 2, 2, nrows // 2, 1, LANES),
            buf(4, 2, 2, 1, LANES),
            buf(4, 4, 2, 1, LANES),
            pltpu.SemaphoreType.DMA((4, 8)),
            pltpu.SemaphoreType.DMA((4, 8)),
            buf(faces * tiles, 1, LANES),
            buf(faces * low, fine_w.shape[2], LANES),
            buf(tiles // low, fine_w.shape[2], LANES),
            pltpu.SemaphoreType.DMA((4, 2)),
        ],
        compiler_params=pltpu.CompilerParams(
            collective_id=0, has_side_effects=True, vmem_limit_bytes=60 * 1024 * 1024
        ),
    )(*operands)
    logits, saliency, grad_f, grad_c = pl.pallas_call(
        write_kernel,
        out_shape=tuple(jax.ShapeDtypeStruct(x.shape, x.dtype) for x in results),
        in_specs=[anywhere] * len(results),
        out_specs=(anywhere,) * len(results),
        scratch_shapes=[
            *[pltpu.VMEM(x.shape, x.dtype) for x in results],
            pltpu.SemaphoreType.DMA((2, len(results))),
        ],
        compiler_params=pltpu.CompilerParams(vmem_limit_bytes=60 * 1024 * 1024),
    )(*results)
    return logits.reshape(nmaps), saliency, grad_f, grad_c


def solution(mesh):
    in_specs = (P(None, None, "face", "tile"), P(), P(), P(), P(), P(), P(), P(), P())
    out_specs = (P(), P(None, None, "face", "tile"), P(), P())
    body = functools.partial(on_device, mesh.shape["face"], mesh.shape["tile"])
    return jax.shard_map(body, mesh=mesh, in_specs=in_specs, out_specs=out_specs, check_vma=False)
```

```python
import functools

import jax
import jax.numpy as jnp
from jax import lax
from jax.experimental import pallas as pl
from jax.experimental.pallas import tpu as pltpu
from jax.sharding import PartitionSpec as P

f32 = jnp.float32
bf16 = jnp.bfloat16
exact = lax.Precision.HIGHEST
MESH = pl.DeviceIdType.MESH
LANES = 128
HALF = 64
UP, DOWN, LEFT, RIGHT, UL, UR, DL, DR = range(8)


def mm(a, b, ca=1, cb=0, precision=exact):
    return lax.dot_general(
        a, b, (((ca,), (cb,)), ((), ())), precision=precision, preferred_element_type=f32
    )


def split(x):
    high = x.astype(bf16)
    return high, (x - high.astype(f32)).astype(bf16)


def mm3(a, b, ca=1, cb=0):
    (ah, al), (bh, bl) = a, b
    left = jnp.concatenate([ah, al, ah], axis=ca)
    right = jnp.concatenate([bh, bh, bl], axis=cb)
    return mm(left, right, ca, cb, None)


def iota(shape, dim):
    return lax.broadcasted_iota(jnp.int32, shape, dim)


def onehot(cond):
    return jnp.where(cond, 1.0, 0.0).astype(f32)


def swap(x):
    return pltpu.roll(x, HALF, axis=x.ndim - 1)


def pick(flag, yes, no):
    return flag * yes + (1.0 - flag) * no


def from_left(x, edge):
    axis = x.ndim - 2
    return jnp.where(iota(x.shape, axis) == 0, edge, pltpu.roll(x, 1, axis=axis))


def from_right(x, edge):
    axis = x.ndim - 2
    n = x.shape[axis]
    return jnp.where(iota(x.shape, axis) == n - 1, edge, pltpu.roll(x, n - 1, axis=axis))


def beside(x, left, right, fine):
    if not fine:
        return from_left(x, left) + from_right(x, right)
    s = swap(x)
    even = iota(x.shape, x.ndim - 1) < HALF
    return s + jnp.where(even, from_left(s, swap(left)), from_right(s, swap(right)))


def lap_row(ref, r, up, down, left, right, fine):
    above = up if r == 0 else ref[r - 1]
    below = down if r == ref.shape[0] - 1 else ref[r + 1]
    return -0.25 * (above + below + beside(ref[r], left, right, fine))


def lane_block(shape, size):
    return (iota(shape, len(shape) - 1) % HALF) // size


def pack_input(size, near, far):
    pair = near + pltpu.roll(far, size, axis=1)
    n = pair.shape[0] // 2
    return pair[:n] + pltpu.roll(pair[n:], 2 * size, axis=1)


def unpack_input(size, packed):
    def block(i):
        here = packed if i == 0 else pltpu.roll(packed, LANES - i * size, axis=1)
        return jnp.where(lane_block(here.shape, size) == 0, here, 0.0)

    near = jnp.concatenate([block(0), block(2)], axis=0)
    far = jnp.concatenate([block(1), block(3)], axis=0)
    return near, far


def pack_pooled(near, far):
    low = iota(near.shape, 1) < HALF
    return jnp.where(low, near + swap(near), far + swap(far))


def unpack_pooled(packed):
    low = iota(packed.shape, 1) < HALF
    return jnp.where(low, packed, 0.0), jnp.where(low, 0.0, packed)


def pack_mixed(size, near, far):
    return jnp.where(
        lane_block(near.shape, size) == 3, pltpu.roll(far, size, axis=1), near
    )


def unpack_mixed(size, packed):
    return packed, pltpu.roll(packed, LANES - size, axis=1)


class Exchange:
    def __init__(self, field, bufs, send_sem, recv_sem, place, fine, pack, unpack):
        self.field, self.place, self.fine = field, place, fine
        self.pack, self.unpack = pack, unpack
        self.row_send, self.row_recv = bufs[:2]
        self.col_send, self.col_recv, self.end_send, self.end_recv = bufs[2:]
        self.send_sem, self.recv_sem = send_sem, recv_sem

    def start(self):
        field, (face, tile, faces, tiles) = self.field, self.place
        nrows, ncols, _ = field.shape
        up, down = lax.rem(face + faces - 1, faces), lax.rem(face + 1, faces)
        left, right = lax.rem(tile + tiles - 1, tiles), lax.rem(tile + 1, tiles)
        copies = [None] * 8

        def send(way, src, dst, target):
            copies[way] = pltpu.make_async_remote_copy(
                src_ref=src,
                dst_ref=dst,
                send_sem=self.send_sem.at[way],
                recv_sem=self.recv_sem.at[way],
                device_id=target,
                device_id_type=MESH,
            )
            copies[way].start()

        if self.pack is None:
            send(UP, field.at[pl.ds(0, 2)], self.row_recv.at[1], (up, tile))
            send(DOWN, field.at[pl.ds(nrows - 2, 2)], self.row_recv.at[0], (down, tile))
        else:
            self.row_send[0] = self.pack(field[0], field[1])
            send(UP, self.row_send.at[0], self.row_recv.at[1], (up, tile))
            self.row_send[1] = self.pack(field[nrows - 1], field[nrows - 2])
            send(DOWN, self.row_send.at[1], self.row_recv.at[0], (down, tile))
        for side, row in ((0, 0), (1, nrows - 1)):
            self.end_send[side, 0] = field[row, 0:1, :]
            self.end_send[side, 1] = field[row, ncols - 1 : ncols, :]
        send(UL, self.end_send.at[0], self.end_recv.at[3], (up, left))
        send(UR, self.end_send.at[0], self.end_recv.at[2], (up, right))
        send(DL, self.end_send.at[1], self.end_recv.at[1], (down, left))
        send(DR, self.end_send.at[1], self.end_recv.at[0], (down, right))
        width = self.col_send.shape[1]
        for w in range(width):
            self.col_send[0, w] = field[:, w : w + 1, :]
            self.col_send[1, w] = field[:, ncols - 1 - w : ncols - w, :]
        send(LEFT, self.col_send.at[0], self.col_recv.at[1], (face, left))
        send(RIGHT, self.col_send.at[1], self.col_recv.at[0], (face, right))
        self.copies = copies

    def rows(self, side):
        got = self.row_recv[side]
        if self.pack is None:
            return (got[1], got[0]) if side == 0 else (got[0], got[1])
        return self.unpack(got)

    def turn(self, x):
        return swap(x) if self.fine else x

    def outer(self, flags, rows, end_left, end_right):
        flag_left, flag, flag_right = flags
        ncols = rows[0].shape[0]
        at = (ncols, 2 * ncols)
        mirror = onehot(iota(at, 0) + iota(at, 1) % ncols == ncols - 1).astype(bf16)
        pair = jnp.concatenate(split(jnp.concatenate(rows, axis=1)), axis=0)
        turned = mm(mirror, pair, 1, 0, None)
        rows = [
            pick(flag, self.turn(turned[:, LANES * i : LANES * (i + 1)]), rows[i]) for i in range(2)
        ]
        row_left = pick(flag, self.turn(end_right[0]), end_left[1])
        row_right = pick(flag, self.turn(end_left[1]), end_right[0])
        col_left = pick(flag_left, self.turn(end_left[0]), end_left[1])
        col_right = pick(flag_right, self.turn(end_right[1]), end_right[0])
        return rows, row_left, row_right, col_left, col_right

    def finish(self, flags_up, flags_down, first_ref, emit, mix=None):
        for copy in self.copies:
            copy.wait()
        fine, x = self.fine, self.field
        nrows, ncols, _ = x.shape
        ends = self.end_recv[...]
        (u1, u2), ul, ur, lu, ru = self.outer(flags_up, self.rows(0), ends[0], ends[1])
        (d1, d2), dl, dr, ld, rd = self.outer(flags_down, self.rows(1), ends[2], ends[3])
        lefts, rights = self.col_recv[0], self.col_recv[1]

        def through(x, first):
            return first if mix is None else mix(x, first)

        for r in range(nrows):
            first = lap_row(x, r, u1, d1, lefts[0, r], rights[0, r], fine)
            first_ref[r] = through(x[r], first)
        first_u = through(u1, -0.25 * (u2 + x[0] + beside(u1, ul, ur, fine)))
        first_d = through(d1, -0.25 * (d2 + x[nrows - 1] + beside(d1, dl, dr, fine)))
        if fine:
            along_l = swap(lefts[0]) + swap(x[:, 0:1, :])
            along_r = swap(rights[0]) + swap(x[:, ncols - 1 : ncols, :])
        else:
            along_l = lefts[1] + x[:, 0:1, :]
            along_r = rights[1] + x[:, ncols - 1 : ncols, :]

        def edge(col, over, under, along):
            above = jnp.concatenate([over[None], col[:-1]], axis=0)
            below = jnp.concatenate([col[1:], under[None]], axis=0)
            return through(col, -0.25 * (above + below + along))

        first_l = edge(lefts[0], lu, ld, along_l)
        first_r = edge(rights[0], ru, rd, along_r)
        for r in range(nrows):
            second = lap_row(first_ref, r, first_u, first_d, first_l[r], first_r[r], fine)
            emit(r, x[r], first_ref[r], second)


class GroupSum:
    def __init__(self, slots, sems, me, visit):
        self.slots, self.sems, self.me, self.visit = slots, sems, me, visit
        self.count = slots.shape[0]

    def start(self, value):
        mine = self.slots.at[self.me]
        mine[...] = value

        def send(device):
            pltpu.make_async_remote_copy(
                src_ref=mine,
                dst_ref=mine,
                send_sem=self.sems.at[0],
                recv_sem=self.sems.at[1],
                device_id=device,
                device_id_type=MESH,
            ).start()

        self.visit(send)

    def finish(self):
        others = self.slots.at[pl.ds(0, self.count - 1)]
        pltpu.make_async_copy(others, others, self.sems.at[1]).wait()
        pltpu.make_async_copy(others, others, self.sems.at[0]).wait()
        return jnp.sum(self.slots[...], axis=0)


def ring(me, count, device_of):
    def visit(act):
        def step(k, _):
            act(device_of(lax.rem(me + k, count)))
            return 0

        if count <= 8:
            for k in range(1, count):
                step(k, 0)
        else:
            lax.fori_loop(1, count, step, 0)

    return visit


def write_kernel(*refs):
    count = len(refs) // 3
    sources, targets, held, sems = refs[:count], refs[count : 2 * count], refs[2 * count : -1], refs[-1]
    loads = [pltpu.make_async_copy(sources[i], held[i], sems.at[0, i]) for i in range(count)]
    stores = [pltpu.make_async_copy(held[i], targets[i], sems.at[1, i]) for i in range(count)]
    for load in loads:
        load.start()
    for load, store in zip(loads, stores):
        load.wait()
        store.start()
    for store in stores:
        store.wait()


def kernel(
    faces,
    tiles,
    *refs,
):
    inputs, outputs, held, made = refs[:9], refs[9:13], refs[13:22], refs[22:26]
    input_sems, output_sems, work = refs[26], refs[27], refs[28:]
    loads = [
        pltpu.make_async_copy(inputs[i], held[i], input_sems.at[i]) for i in range(len(inputs))
    ]
    for load in loads:
        load.start()
    stores = [
        pltpu.make_async_copy(made[i], outputs[i], output_sems.at[i]) for i in range(len(outputs))
    ]
    run(faces, tiles, loads, stores, *held, *made, *work)
    for store in stores:
        store.wait()


def run(
    faces,
    tiles,
    loads,
    stores,
    maps_ref,
    params_ref,
    labels_ref,
    flip_ref,
    fine_ref,
    coarse_ref,
    feature_ref,
    param_w_ref,
    out_w_ref,
    logits_ref,
    sal_ref,
    grad_f_ref,
    grad_c_ref,
    x0_ref,
    first0_ref,
    split0_ref,
    pre0_ref,
    sig0_ref,
    x1_ref,
    first1_ref,
    split1_ref,
    d1_ref,
    split_d1_ref,
    d0_ref,
    split_d0_ref,
    flat_ref,
    input_rows_send,
    input_rows_recv,
    pooled_rows_send,
    pooled_rows_recv,
    mixed_rows_send,
    mixed_rows_recv,
    deep_rows_recv,
    fine_col_send,
    fine_col_recv,
    coarse_col_send,
    coarse_col_recv,
    end_send,
    end_recv,
    halo_send,
    halo_recv,
    feature_near,
    feature_high,
    near_slots,
    high_slots,
    sum_sems,
):
    face, tile = lax.axis_index("face"), lax.axis_index("tile")
    place = (face, tile, faces, tiles)
    devices = faces * tiles
    nbins, nch0 = fine_ref.shape[1:]
    nch1 = coarse_ref.shape[2]
    nmaps = params_ref.shape[1]
    order = fine_ref.shape[0]
    nrows = maps_ref.shape[2]
    ncols = maps_ref.shape[3] // 2
    fields = nmaps * nbins
    pooled = float(nrows // 2 * ncols * devices)

    low = tiles // high_slots.shape[0]
    tile_high, tile_low = lax.div(tile, low), lax.rem(tile, low)
    my_near = face * low + tile_low

    def near_device(j):
        return lax.div(j, low), tile_high * low + lax.rem(j, low)

    def high_device(j):
        return face, j * low + tile_low

    visit_near = ring(my_near, near_slots.shape[0], near_device)
    visit_high = ring(tile_high, high_slots.shape[0], high_device)

    def group_sums(near, high, i):
        return [
            GroupSum(near, sum_sems.at[i], my_near, visit_near),
            GroupSum(high, sum_sems.at[i + 1], tile_high, visit_high),
        ]

    barrier = pltpu.get_barrier_semaphore()

    def greet(device):
        pl.semaphore_signal(barrier, inc=1, device_id=device, device_id_type=MESH)

    up, down = lax.rem(face + faces - 1, faces), lax.rem(face + 1, faces)
    left, right = lax.rem(tile + tiles - 1, tiles), lax.rem(tile + 1, tiles)
    halo = [(f, t) for f in (up, down) for t in (left, tile, right)]
    halo += [(face, left), (face, right)]
    for device in halo:
        greet(device)
    visit_near(greet)
    visit_high(greet)
    greeted = len(halo) + near_slots.shape[0] - 1 + high_slots.shape[0] - 1

    square = (LANES, LANES)
    ri, ci = iota(square, 0), iota(square, 1)
    even_first = onehot(ri == 2 * (ci % HALF) + ci // HALF).astype(bf16)
    loads[0].wait()
    flat_ref[...] = mm(maps_ref[...].reshape(-1, LANES), even_first, 1, 0, None)
    low_half = iota((fields, LANES), 1) < HALF
    zero = jnp.zeros((HALF - fields, LANES), f32)

    def row_of(r):
        return flat_ref.at[pl.ds(r, fields, stride=nrows)]

    for r in range(0, nrows, 2):
        one, two = row_of(r)[...], row_of(r + 1)[...]
        even = jnp.where(low_half, one, swap(two))
        odd = jnp.where(low_half, swap(one), two)
        both = jnp.concatenate([even, zero, odd, zero], axis=0)
        x0_ref[pl.ds(r, 2)] = both.T.reshape(2, ncols, LANES)

    pl.semaphore_wait(barrier, greeted)

    def exchange(i, field, rows, fine, pack, unpack):
        cols = (fine_col_send, fine_col_recv) if fine else (coarse_col_send, coarse_col_recv)
        bufs = rows + tuple(c.at[i // 2] for c in cols) + (end_send.at[i], end_recv.at[i])
        return Exchange(field, bufs, halo_send.at[i], halo_recv.at[i], place, fine, pack, unpack)

    ex0 = exchange(
        0,
        x0_ref,
        (input_rows_send, input_rows_recv),
        True,
        functools.partial(pack_input, fields),
        functools.partial(unpack_input, fields),
    )
    ex0.start()
    for load in loads[1:]:
        load.wait()

    below = lax.rem(face + 1, faces)
    spots = (lax.rem(tile + tiles - 1, tiles), tile, lax.rem(tile + 1, tiles))
    flags_up = [jnp.where(flip_ref[face, s] == 1, 1.0, 0.0).astype(f32) for s in spots]
    flags_down = [jnp.where(flip_ref[below, s] == 1, 1.0, 0.0).astype(f32) for s in spots]

    at_ch0 = onehot(iota((nch0, LANES), 1) % nch0 == iota((nch0, LANES), 0)).astype(bf16)
    at_ch1 = onehot(iota((nch1, LANES), 1) % nch1 == iota((nch1, LANES), 0)).astype(bf16)

    def spread(left, terms, right, ca):
        width = terms[0].shape[1]
        rows = mm(left, jnp.concatenate(terms, axis=1), ca, 0, None).astype(bf16)
        rows = [rows[:, i * width : (i + 1) * width] for i in range(len(terms))]
        if right is None:
            return rows
        full = mm(jnp.concatenate(rows, axis=0), right, 1, 0, None)
        return [full[i * LANES : (i + 1) * LANES] for i in range(len(terms))]

    mask0 = onehot(
        (ri // HALF == ci // HALF)
        & ((ri % HALF) // fields < order)
        & ((ri % fields) // nbins == (ci % HALF) // nch0)
    )
    rf, cf = iota((LANES, order * nbins), 0), iota((LANES, order * nbins), 1)
    at_term = onehot(((rf % HALF) // fields == cf // nbins) & (rf % nbins == cf % nbins))
    fine_w = jnp.concatenate([fine_ref[k] for k in range(order)], axis=0)
    mixing = spread(at_term.astype(bf16), split(fine_w), at_ch0, 1)
    mixing = [(mask0 * m).astype(bf16) for m in mixing]
    head_mask = onehot(iota((nmaps, LANES), 0) == iota((nmaps, LANES), 1) // nch1)
    from_params = mm(params_ref[...], param_w_ref[...], 0, 0)
    spot = iota((nmaps, nmaps), 0) == iota((nmaps, nmaps), 1)
    labels = jnp.sum(
        jnp.where(spot, labels_ref[...].astype(f32), 0.0), axis=1, keepdims=True
    )

    def beside_lows(weights, axis):
        highs, lows = [jnp.concatenate(w, axis=axis) for w in zip(*weights)]
        return jnp.concatenate(
            [
                jnp.concatenate([highs, highs], axis=axis),
                jnp.concatenate([lows, jnp.zeros_like(lows)], axis=axis),
            ],
            axis=1 - axis,
        )

    def folded(x):
        return x[:, :LANES] + x[:, LANES:]

    def put(ref, r, places, x):
        for place, part in zip(places, split(x)):
            ref[r * ncols : (r + 1) * ncols, place * LANES : (place + 1) * LANES] = part

    def soft(v):
        small = jnp.exp(-jnp.abs(v))
        sig = jnp.where(v >= 0, 1.0, small) / (1.0 + small)
        return jnp.maximum(v, 0.0) + jnp.log1p(small), sig

    mix_forward, mix_back = beside_lows([mixing], 0), beside_lows([mixing], 1)

    def emit_fine(r, x, first, outer):
        second = 2.0 * outer - x
        terms = x + pltpu.roll(first, fields, axis=1) + pltpu.roll(second, 2 * fields, axis=1)
        put(split0_ref, r, (0, 1), terms)

    ex0.finish(flags_up, flags_down, first0_ref, emit_fine)
    pre0_ref[...] = folded(mm(split0_ref[...], mix_forward, 1, 0, None)).reshape(pre0_ref.shape)
    for r in range(0, nrows, 2):
        acts = []
        for q in (r, r + 1):
            act, sig = soft(pre0_ref[q])
            sig0_ref[q] = 0.25 * sig
            acts.append(act)
        x1_ref[r // 2] = 0.25 * (acts[0] + acts[1])

    ex1 = exchange(
        1, x1_ref, (pooled_rows_send, pooled_rows_recv), False, pack_pooled, unpack_pooled
    )
    ex1.start()
    mask1 = onehot((ri % HALF) // nch0 == ci // nch1)
    terms = [t for k in range(order) for t in split(coarse_ref[k])]
    terms = [(mask1 * t).astype(bf16) for t in spread(at_ch0, terms, at_ch1, 0)]
    w1 = [terms[2 * k : 2 * k + 2] for k in range(order)]
    wf = spread(at_ch1, split(feature_ref[...]), None, 0)
    coarse_forward = beside_lows(w1, 0)

    def emit_coarse(r, x, first, outer):
        for k, term in enumerate((x, first, 2.0 * outer - x)):
            put(split1_ref, r, (k, order + k), term)

    ex1.finish(flags_up, flags_down, first1_ref, emit_coarse)
    pre1 = folded(mm(split1_ref[...], coarse_forward, 1, 0, None))
    act_sum = jnp.zeros((ncols, LANES), f32)
    for r in range(nrows // 2):
        act, sig = soft(pre1[r * ncols : (r + 1) * ncols])
        act_sum = act_sum + act
        d1_ref[r] = sig
    feature_sums = group_sums(feature_near, feature_high, 3)
    feature_sums[0].start(jnp.sum(act_sum, axis=0, keepdims=True))

    ex2 = exchange(2, d1_ref, (None, deep_rows_recv), False, None, None)
    ex2.start()

    row, lane = iota((nch0, LANES), 0), iota((nch0, LANES), 1)
    for r in range(nrows // 2):
        put(split_d1_ref, r, (0, 1), d1_ref[r])
    feature_sums[1].start(feature_sums[0].finish())
    products = mm(split1_ref[...], split_d1_ref[...], 0, 0, None)
    unscaled = []
    for k in range(order):
        full = folded(products[k * LANES : (k + 1) * LANES])
        full = full + products[(order + k) * LANES : (order + k + 1) * LANES, :LANES]
        unscaled.append(jnp.sum((mask1 * full).reshape(-1, nch0, LANES), axis=0))

    features = feature_sums[1].finish() / pooled
    hidden = jnp.tanh(mm3(split(head_mask * features), wf) + from_params)
    logits = jnp.sum(hidden * out_w_ref[...], axis=1, keepdims=True)
    logits_ref[...] = jnp.sum(jnp.where(spot, logits, 0.0), axis=0, keepdims=True)
    stores[0].start()
    dlogit = 1.0 / (1.0 + jnp.exp(-logits)) - labels
    dhidden = dlogit * out_w_ref[...] * (1.0 - hidden * hidden)
    dfeatures = jnp.sum(head_mask * mm3(split(dhidden), wf, 1, 1), axis=0, keepdims=True)
    scale = dfeatures / pooled
    scaled = [split(scale * (h.astype(f32) + l.astype(f32))) for h, l in w1]

    coarse_back = beside_lows(scaled, 1)
    ex2.finish(flags_up, flags_down, first1_ref, emit_coarse)
    dx1 = folded(mm(split1_ref[...], coarse_back, 1, 1, None))
    for r in range(nrows):
        put(split_d0_ref, r, (0, 1), dx1[r // 2 * ncols : (r // 2 + 1) * ncols] * sig0_ref[r])

    d0_ref[...] = folded(mm(split_d0_ref[...], mix_back, 1, 1, None)).reshape(d0_ref.shape)
    ex3 = exchange(
        3,
        d0_ref,
        (mixed_rows_send, mixed_rows_recv),
        True,
        functools.partial(pack_mixed, fields),
        functools.partial(unpack_mixed, fields),
    )
    ex3.start()
    grads = jnp.zeros((nch0, LANES), f32)
    for k in range(order):
        part = scale * unscaled[k]
        shift = LANES // 2
        while shift >= nch1:
            part = part + pltpu.roll(part, shift, axis=1)
            shift //= 2
        grads = jnp.where(lane // nch1 == k, part, grads)
    products = mm(split0_ref[...], split_d0_ref[...], 0, 0, None)
    full = mask0 * (folded(products[:LANES]) + products[LANES:, :LANES])
    for k in range(order):
        start = k * fields
        part = full[start : start + fields] + full[HALF + start : HALF + start + fields]
        shift = fields // 2
        while shift >= nbins:
            part = part + pltpu.roll(part, shift, axis=0)
            shift //= 2
        shift = LANES // 2
        while shift >= nch0:
            part = part + pltpu.roll(part, shift, axis=1)
            shift //= 2
        here = (row // nbins == k) & (lane // nch0 == order * nch1 // nch0)
        grads = jnp.where(here, part, grads)

    sums = group_sums(near_slots, high_slots, 1)
    sums[0].start(grads)
    def mix(x, first):
        return x + 2.0 * pltpu.roll(first, LANES - fields, axis=first.ndim - 1)

    block = lane_block((ncols, LANES), fields)
    pixels = float(nrows * faces * 2 * ncols * tiles)

    def emit_back(r, x, first, outer):
        sig0_ref[r] = pixels * jnp.where(block == 0, x, jnp.where(block == 1, outer, -x))

    sums[1].start(sums[0].finish())
    ex3.finish(flags_up, flags_down, first0_ref, emit_back, mix)
    for r in range(0, nrows, 2):
        both = sig0_ref[pl.ds(r, 2)].reshape(LANES, LANES).T
        even, odd = [
            both[h : h + fields] + both[h + fields : h + 2 * fields] + both[h + 2 * fields : h + 3 * fields]
            for h in (0, HALF)
        ]
        row_of(r)[...] = jnp.where(low_half, even, swap(odd))
        row_of(r + 1)[...] = jnp.where(low_half, swap(even), odd)
    woven = jnp.concatenate(split(flat_ref[...]), axis=1)
    twice = jnp.concatenate([even_first, even_first], axis=1)
    sal_ref[...] = mm(woven, twice, 1, 1, None).reshape(sal_ref.shape)
    stores[1].start()
    grads = sums[1].finish()
    for k in range(order):
        grad_c_ref[k] = grads[:, k * nch1 : (k + 1) * nch1]
        start = order * nch1
        grad_f_ref[k] = grads[k * nbins : (k + 1) * nbins, start : start + nch0]
    stores[2].start()
    stores[3].start()


def on_device(faces, tiles, maps, params, labels, flip, fine_w, coarse_w, feature_w, param_w, out_w):
    nmaps, nbins, nrows, width = maps.shape
    ncols = width // 2
    low = 1
    while low * low < tiles:
        low *= 2
    fine = (nrows, ncols, LANES)
    coarse = (nrows // 2, ncols, LANES)

    def buf(*shape):
        return pltpu.VMEM(shape, f32)

    operands = (
        maps,
        params.T,
        labels.reshape(1, nmaps),
        flip,
        fine_w,
        coarse_w,
        feature_w,
        param_w,
        out_w.reshape(1, -1),
    )
    held = [pltpu.VMEM(x.shape, x.dtype) for x in operands]
    held[3] = pltpu.SMEM(flip.shape, flip.dtype)
    anywhere = pl.BlockSpec(memory_space=pl.ANY)
    shapes = ((1, nmaps), maps.shape, fine_w.shape, coarse_w.shape)
    results = pl.pallas_call(
        functools.partial(kernel, faces, tiles),
        out_shape=tuple(jax.ShapeDtypeStruct(shape, f32) for shape in shapes),
        in_specs=[anywhere] * len(operands),
        out_specs=(anywhere,) * 4,
        scratch_shapes=[
            *held,
            *[buf(*shape) for shape in shapes],
            pltpu.SemaphoreType.DMA((len(operands),)),
            pltpu.SemaphoreType.DMA((len(shapes),)),
            buf(*fine),
            buf(*fine),
            pltpu.VMEM((nrows * ncols, 2 * LANES), bf16),
            buf(*fine),
            buf(*fine),
            buf(*coarse),
            buf(*coarse),
            pltpu.VMEM((nrows // 2 * ncols, 2 * fine_w.shape[0] * LANES), bf16),
            buf(*coarse),
            pltpu.VMEM((nrows // 2 * ncols, 2 * LANES), bf16),
            buf(*fine),
            pltpu.VMEM((nrows * ncols, 2 * LANES), bf16),
            buf(nmaps * nbins * nrows, width),
            buf(2, ncols // 2, LANES),
            buf(2, ncols // 2, LANES),
            buf(2, ncols, LANES),
            buf(2, ncols, LANES),
            buf(2, ncols, LANES),
            buf(2, ncols, LANES),
            buf(2, 2, ncols, LANES),
            buf(2, 2, 1, nrows, 1, LANES),
            buf(2, 2, 1, nrows, 1, LANES),
            buf(2, 2, 2, nrows // 2, 1, LANES),
            buf(2, 2, 2, nrows // 2, 1, LANES),
            buf(4, 2, 2, 1, LANES),
            buf(4, 4, 2, 1, LANES),
            pltpu.SemaphoreType.DMA((4, 8)),
            pltpu.SemaphoreType.DMA((4, 8)),
            buf(faces * low, 1, LANES),
            buf(tiles // low, 1, LANES),
            buf(faces * low, fine_w.shape[2], LANES),
            buf(tiles // low, fine_w.shape[2], LANES),
            pltpu.SemaphoreType.DMA((5, 2)),
        ],
        compiler_params=pltpu.CompilerParams(
            collective_id=0, has_side_effects=True, vmem_limit_bytes=60 * 1024 * 1024
        ),
    )(*operands)
    logits, saliency, grad_f, grad_c = pl.pallas_call(
        write_kernel,
        out_shape=tuple(jax.ShapeDtypeStruct(x.shape, x.dtype) for x in results),
        in_specs=[anywhere] * len(results),
        out_specs=(anywhere,) * len(results),
        scratch_shapes=[
            *[pltpu.VMEM(x.shape, x.dtype) for x in results],
            pltpu.SemaphoreType.DMA((2, len(results))),
        ],
        compiler_params=pltpu.CompilerParams(vmem_limit_bytes=60 * 1024 * 1024),
    )(*results)
    return logits.reshape(nmaps), saliency, grad_f, grad_c


def solution(mesh):
    in_specs = (P(None, None, "face", "tile"), P(), P(), P(), P(), P(), P(), P(), P())
    out_specs = (P(), P(None, None, "face", "tile"), P(), P())
    body = functools.partial(on_device, mesh.shape["face"], mesh.shape["tile"])
    return jax.shard_map(body, mesh=mesh, in_specs=in_specs, out_specs=out_specs, check_vma=False)
```
